512 devices in a mesh: gx: 64 (over z, x), gy: 4 (over y), ma: 2 (over core).
Axes of the slice: x: 4, y: 4, z: 16, core: 2. Of those that a mesh axis runs over, the one named last changes fastest.
Arguments:
- permeability: float32 [1024, 128, 128], P(('ma', 'gx'), 'gy'), parts along dimension 0, may hold values from 0.05 to 20
- storage: float32 [1024, 128, 128], P(('ma', 'gx'), 'gy'), parts along dimension 0, may hold values from 0.05 to 0.5
- source_term: float32 [1024, 128, 128], P(('ma', 'gx'), 'gy'), parts along dimension 0, may hold values from -24 to 24
Outputs:
- pressure: float32 [1024, 128, 128], P(('ma', 'gx'), 'gy'), parts along dimension 0
- residual: float32 [1024, 128, 128], P(('ma', 'gx'), 'gy'), parts along dimension 0
The draws below stay inside these ranges and needn't reach their ends.
There are 2 independent parts, one for each index of `ma`. The reference program is written for one: setup_inputs(seed, part) draws one part's arguments, and reference() takes and returns one part's arrays. A program takes and returns all parts, laid end to end along the dimension named above; each array names one. Nothing has to cross between parts.
All inputs are finite; a program needn't handle non-finite values.
Results may differ from the reference program's by a relative error of at most 0.00014.
Values sent between devices are 32-bit elements; how exact they have to be, the bound alone decides.
No kernel may reach another device: no remote copies, remote signals or barrier semaphores. Data moves between devices by JAX's collectives and lax.ppermute only.
A program may use at most 64 MiB of HBM per device.

```python
import math
import jax
import jax.numpy as jnp

LEVELS = 4
COARSE = 8
NX = 512
NY = 128
NZ = 128


def steps_of(own_key, extent, pieces, smallest, largest):
    level = 1.0
    for dim, parts in pieces:
        draws = jax.random.uniform(jax.random.fold_in(jax.random.fold_in(own_key, 6), dim), (parts,), jnp.float32, smallest / len(pieces), largest / len(pieces))
        level = level * jnp.repeat(jnp.exp(draws), extent[dim] // parts).reshape((-1,) + (1,) * (len(extent) - 1 - dim))
    return level


def centred(stream_key, extent, width, reach, pieces=(), held_as=jnp.bfloat16):
    drawn = jax.random.normal(stream_key, extent, jnp.float32) * width
    if len(pieces) > 0:
        drawn = steps_of(stream_key, extent, pieces, -0.22, 0.18) * drawn
    return jnp.clip(drawn, min=-reach, max=reach).astype(held_as)


def setup_inputs(seed: int = 0, part: int = 0) -> dict:
    seeds = jax.random.split(jax.random.key(seed), 4)
    part_splits = jax.random.split(jax.random.fold_in(seeds[3], part), 4)
    permeability = jnp.clip(jnp.exp(math.log(20.0) - 5.9914645 * jax.random.uniform(part_splits[0], (NX, NY, NZ), jnp.float32) ** steps_of(part_splits[0], (NX, NY, NZ), ((0, 64), (1, 4)), -0.2, 0.2)), 0.05, 20.0)
    storage = jnp.clip(jnp.exp(math.log(0.5) - 2.3025851 * jax.random.uniform(part_splits[1], (NX, NY, NZ), jnp.float32) ** steps_of(part_splits[1], (NX, NY, NZ), ((0, 64), (1, 4)), -0.2, 0.2)), 0.05, 0.5)
    source_term = centred(part_splits[2], (NX, NY, NZ), 4.0, 24.0, ((0, 64), (1, 4)), jnp.float32)
    return dict(permeability=permeability, storage=storage, source_term=source_term)


OMEGA = 0.7


def neighbours_of(padded):
    return (padded[:-2, 1:-1, 1:-1], padded[2:, 1:-1, 1:-1], padded[1:-1, :-2, 1:-1],
            padded[1:-1, 2:, 1:-1], padded[1:-1, 1:-1, :-2], padded[1:-1, 1:-1, 2:])


def transmissibility(padded_perm, store_now, coarsening):
    factor = 2.0 ** coarsening
    middle = padded_perm[1:-1, 1:-1, 1:-1]
    transmit = tuple(factor * 2.0 * middle * beside / (middle + beside) for beside in neighbours_of(padded_perm))
    diagonal = store_now + transmit[0] + transmit[1] + transmit[2] + transmit[3] + transmit[4] + transmit[5]
    return transmit, diagonal


def operate(padded, transmit, store_now):
    centre = padded[1:-1, 1:-1, 1:-1]
    beside_all = neighbours_of(padded)
    outflow = transmit[0] * (centre - beside_all[0])
    for position in range(1, 6):
        outflow = outflow + transmit[position] * (centre - beside_all[position])
    return store_now * centre + outflow


def restrict(field):
    length_x, length_y, length_z = field.shape
    return field.reshape(length_x // 2, 2, length_y // 2, 2, length_z // 2, 2).sum(axis=(1, 3, 5))


def prolong(field):
    length_x, length_y, length_z = field.shape
    spread_out = jnp.broadcast_to(field[:, None, :, None, :, None], (length_x, 2, length_y, 2, length_z, 2))
    return spread_out.reshape(2 * length_x, 2 * length_y, 2 * length_z)


def relax(iterate, source, transmit, diagonal, store_now):
    return iterate + OMEGA * (source - operate(jnp.pad(iterate, 1), transmit, store_now)) / diagonal


def reference(permeability, storage, source_term):
    operators = []
    perm_now, store_now = permeability, storage
    for coarsening in range(LEVELS):
        transmit, diagonal = transmissibility(jnp.pad(perm_now, 1), store_now, coarsening)
        operators.append((transmit, diagonal, store_now))
        if coarsening < LEVELS - 1:
            perm_now = restrict(perm_now) * 0.125
            store_now = restrict(store_now)

    def cycle(source, coarsening):
        transmit, diagonal, store_here = operators[coarsening]
        iterate = OMEGA * source / diagonal
        if coarsening == LEVELS - 1:
            for sweep_count in range(COARSE - 1):
                iterate = relax(iterate, source, transmit, diagonal, store_here)
            return iterate
        iterate = relax(iterate, source, transmit, diagonal, store_here)
        defect = source - operate(jnp.pad(iterate, 1), transmit, store_here)
        iterate = iterate + prolong(cycle(restrict(defect), coarsening + 1))
        iterate = relax(iterate, source, transmit, diagonal, store_here)
        iterate = relax(iterate, source, transmit, diagonal, store_here)
        return iterate

    pressure = cycle(source_term, 0)
    transmit, diagonal, store_here = operators[0]
    residual = source_term - operate(jnp.pad(pressure, 1), transmit, store_here)
    return pressure, residual
```

```python
import jax
import jax.numpy as jnp
from jax import lax
from jax.experimental import pallas as pl
from jax.experimental.pallas import tpu as pltpu
from jax.sharding import PartitionSpec as P

OMEGA = 0.7
COARSE = 8
F32 = jnp.float32


def lanes(like):
    return lax.broadcasted_iota(jnp.int32, like.shape, 1)


def rows(like):
    return lax.broadcasted_iota(jnp.int32, like.shape, 0)


def roll(v, shift, axis):
    return pltpu.roll(v, shift % v.shape[axis], axis)


def bit(v, b):
    return (lanes(v) & b) == 0


def split(p, b):
    low = bit(p, b)
    return jnp.where(low, p, roll(p, b, 1)), jnp.where(low, roll(p, -b, 1), p)


def pack2(a, b):
    return jnp.where(bit(a, 1), a, b)


def unpack2(p):
    return split(p, 1)


def pack4(a, b, c, d):
    return jnp.where(bit(a, 2), pack2(a, b), pack2(c, d))


def unpack4(p):
    even, odd = split(p, 1)
    a, c = split(even, 2)
    b, d = split(odd, 2)
    return a, b, c, d


def pack8(v):
    return jnp.where(bit(v[0], 4), pack4(*v[:4]), pack4(*v[4:]))


def unpack8(p):
    a, b, c, d = unpack4_pairs(p)
    return a[0], b[0], c[0], d[0], a[1], b[1], c[1], d[1]


def unpack4_pairs(p):
    return tuple(split(q, 4) for q in unpack4(p))


def harmonic(a, b, level):
    return 2.0**level * 2.0 * a * b / jnp.maximum(a + b, 0.01)


class Level:
    def __init__(self, level, whole_y, tx, ty, tz, store, gain):
        self.level, self.whole_y = level, whole_y
        self.tx, self.ty, self.tz, self.store, self.gain = tx, ty, tz, store, gain
        self.w = 2**level

    def build(self, perm, first, last, origin=None, extent=None):
        for p in range(first, last + 2):
            face = harmonic(perm[p], perm[p - 1], self.level)
            if origin is not None:
                at = origin + p
                face = face * jnp.where((at == 0) | (at == extent), 0.0, 1.0)
            self.tx[p] = face
        for p in range(first, last + 1):
            k = perm[p]
            ty = harmonic(k, roll(k, 1, 0), self.level)
            if self.whole_y:
                ty = jnp.where(rows(k) < 1, 0.0, ty)
            tz = jnp.where(lanes(k) < self.w, 0.0, harmonic(k, roll(k, self.w, 1), self.level))
            self.ty[p] = ty
            self.tz[p] = tz
            d = (
                self.store[p] + self.tx[p] + self.tx[p + 1] + ty + roll(ty, -1, 0)
                + tz + roll(tz, -self.w, 1)
            )
            self.gain[p] = OMEGA / jnp.maximum(d, 0.01)

    def apply(self, v, first, last, use):
        low = self.tx[first] * (v[first] - v[first - 1])
        for p in range(first, last + 1):
            here = v[p]
            high = self.tx[p + 1] * (v[p + 1] - here)
            fy = self.ty[p] * (here - roll(here, 1, 0))
            fz = self.tz[p] * (here - roll(here, self.w, 1))
            out = (
                self.store[p] * here + (low - high) + (fy - roll(fy, -1, 0))
                + (fz - roll(fz, -self.w, 1))
            )
            use(p, here, out)
            low = high

    def sweep(self, v, source, first, last):
        def use(p, here, out):
            v[p] = here + self.gain[p] * (source[p] - out)

        self.apply(v, first, last, use)

    def first_sweep(self, v, source, first, last):
        for p in range(first, last + 1):
            v[p] = self.gain[p] * source[p]

    def defect(self, r, v, source, first, last):
        def use(p, here, out):
            r[p] = source[p] - out

        self.apply(v, first, last, use)


def restrict(ref, p, count, level):
    half = count // 2
    t = ref[p, pl.ds(0, half, stride=2), :] + ref[p, pl.ds(1, half, stride=2), :]
    t = t + (ref[p + 1, pl.ds(0, half, stride=2), :] + ref[p + 1, pl.ds(1, half, stride=2), :])
    w = 2**level
    return t + jnp.where(bit(t, w), roll(t, -w, 1), roll(t, w, 1))


def doubled(ref, p, e):
    half = e.shape[0]
    ref[p, pl.ds(0, half, stride=2), :] = e
    ref[p, pl.ds(1, half, stride=2), :] = e


def rows_kernel(k, f, s, xl, xr, up, down):
    zero = jnp.zeros((8, 128), F32)
    sub = rows(zero)

    def planes(p):
        if p < 3:
            kp = lambda sl: xl[p, sl, :]
            fp = (lambda sl: xl[3 + p - 1, sl, :]) if p >= 1 else None
            sp = (lambda sl: xl[5 + p - 1, sl, :]) if p >= 1 else None
        elif p < 11:
            kp = lambda sl: k[p - 3, sl, :]
            fp = lambda sl: f[p - 3, sl, :]
            sp = lambda sl: s[p - 3, sl, :]
        else:
            kp = lambda sl: xr[p - 11, sl, :]
            fp = (lambda sl: xr[3 + p - 11, sl, :]) if p < 13 else None
            sp = (lambda sl: xr[5 + p - 11, sl, :]) if p < 13 else None
        return kp, fp, sp

    last, initial = pl.ds(24, 8), pl.ds(0, 8)
    for p in range(14):
        kp, fp, sp = planes(p)
        fl, sl = (zero, zero) if fp is None else (fp(last), sp(last))
        up[p] = jnp.where(sub >= 5, kp(last), jnp.where(sub >= 3, roll(fl, -3, 0), roll(sl, -5, 0)))
        fi, si = (zero, zero) if fp is None else (fp(initial), sp(initial))
        down[p] = jnp.where(sub < 3, kp(initial), jnp.where(sub < 5, roll(fi, 3, 0), roll(si, 5, 0)))


def fine_kernel(
    k, f, s, xl, xr, above, below, r0, v0, tx, ty, tz, st, gain, msg, ke, fe, ve, re
):
    zero = jnp.zeros((8, 128), F32)
    sub = rows(zero)
    own, edge = pl.ds(0, 32), pl.ds(32, 8)
    for p in range(14):
        a, b = above[p], below[p]
        ke[p, edge, :] = jnp.where(sub < 3, a, jnp.where(sub >= 5, b, 0.0))
        fe[p, edge, :] = jnp.where(
            sub < 2, roll(a, -3, 0), jnp.where(sub >= 6, roll(b, 3, 0), 0.0)
        )
        st[p, edge, :] = jnp.where(
            sub < 2, roll(a, -5, 0), jnp.where(sub >= 6, roll(b, 5, 0), 0.0)
        )
        if p < 3:
            ke[p, own, :] = xl[p]
            if p >= 1:
                fe[p, own, :] = xl[2 + p]
                st[p, own, :] = xl[4 + p]
        elif p < 11:
            ke[p, own, :] = k[p - 3]
            fe[p, own, :] = f[p - 3]
            st[p, own, :] = s[p - 3]
        else:
            ke[p, own, :] = xr[p - 11]
            if p < 13:
                fe[p, own, :] = xr[p - 8]
                st[p, own, :] = xr[p - 6]
    op = Level(0, False, tx, ty, tz, st, gain)
    op.build(ke, 1, 12)
    op.first_sweep(ve, fe, 1, 12)
    op.sweep(ve, fe, 2, 11)
    op.defect(re, ve, fe, 3, 10)
    for p in range(8):
        r0[p] = re[p + 3, own, :]
        v0[p] = ve[p + 3, own, :]
    source = [restrict(re, 3 + 2 * p, 32, 0) for p in range(4)]
    perm = [restrict(ke, 3 + 2 * p, 32, 0) * 0.125 for p in range(4)]
    store = [restrict(st, 3 + 2 * p, 32, 0) for p in range(4)]
    packed = [
        pack2(source[0], source[1]), pack2(source[2], source[3]),
        pack2(perm[0], perm[1]), pack2(perm[2], perm[3]),
        pack2(store[0], store[1]), pack2(store[2], store[3]),
    ]
    tiles = []
    for p in range(8):
        t = jnp.where(sub < 2, re[p + 3, pl.ds(0, 8), :], roll(re[p + 3, pl.ds(24, 8), :], -4, 0))
        tiles.append(t)
    edges = [jnp.where(sub < 4, tiles[p], roll(tiles[p + 4], 4, 0)) for p in range(4)]
    for peer in range(4):
        for i in range(6):
            msg[peer, i] = packed[i]
        for i in range(4):
            msg[peer, 6 + i // 2, pl.ds(8 * (i % 2), 8), :] = edges[i]


def middle_kernel(
    gc, gl, gr, r0, to_left, to_right, r0h, tx, ty, tz, st, gain, v1, r1, ke, fe, de
):
    for block, ref in enumerate((gl, gc, gr)):
        for j in range(4):
            sl = pl.ds(16 * j, 16)
            for half in range(2):
                for target, at in ((fe, 0), (ke, 2), (st, 4)):
                    a, b = unpack2(ref[j, at + half])
                    target[4 * block + 2 * half, sl, :] = a
                    target[4 * block + 2 * half + 1, sl, :] = b
    op = Level(1, True, tx, ty, tz, st, gain)
    op.build(ke, 1, 10)
    op.first_sweep(v1, fe, 1, 10)
    op.sweep(v1, fe, 2, 9)
    op.defect(r1, v1, fe, 3, 8)
    source = [restrict(r1, 4 + 2 * p, 64, 1) for p in range(2)]
    store = [restrict(st, 4 + 2 * p, 64, 1) for p in range(2)]
    perm = [restrict(ke, 2 + 2 * p, 64, 1) * 0.125 for p in range(4)]
    faces = [harmonic(perm[p], perm[p + 1], 2) for p in range(3)]
    for p in range(2):
        k = perm[p + 1]
        fy = jnp.where(rows(k) < 1, 0.0, harmonic(k, roll(k, 1, 0), 2))
        fz = jnp.where(lanes(k) < 4, 0.0, harmonic(k, roll(k, 4, 1), 2))
        de[p] = store[p] + faces[p] + faces[p + 1] + fy + roll(fy, -1, 0) + fz + roll(fz, -4, 1)
    block = (
        pack4(source[0], source[1], perm[1], perm[2]),
        pack4(store[0], store[1], de[0], de[1]),
    )
    edge = pack2(r1[5], r1[6])
    j = lax.axis_index("gy")
    jn, jp = jnp.minimum(j + 1, 3), jnp.maximum(j - 1, 0)
    sub = rows(jnp.zeros((8, 128), F32))
    for p in range(8):
        i = p % 4
        at = (6 + i // 2, pl.ds(8 * (i % 2), 8), slice(None))
        a, b = gc[(jn,) + at], gc[(jp,) + at]
        if p >= 4:
            a, b = roll(a, -4, 0), roll(b, -4, 0)
        r0h[p] = jnp.where(sub < 4, a, roll(b, 4, 0))
    for ref, planes in ((to_left, (0, 1)), (to_right, (6, 7))):
        ref[pl.ds(0, 32), :] = block[0]
        ref[pl.ds(32, 32), :] = block[1]
        ref[pl.ds(64, 64), :] = edge
        for n, p in enumerate(planes):
            ref[pl.ds(128 + 40 * n, 32), :] = r0[p]
            ref[pl.ds(160 + 40 * n, 8), :] = r0h[p]


def coarse_kernel(own, left, right, msg, tx, ty, tz, st, gain, v2, r2, ke, fe, de):
    n = 0
    for ref in (left, own, right):
        for b in range(3):
            a = unpack4(ref[pl.ds(64 * b, 32), :])
            c = unpack4(ref[pl.ds(64 * b + 32, 32), :])
            for half in range(2):
                fe[n + half] = a[half]
                ke[n + half] = a[2 + half]
                st[n + half] = c[half]
                de[n + half] = c[2 + half]
            n += 2
    op = Level(2, True, tx, ty, tz, st, gain)
    i = lax.axis_index("gx")
    op.build(ke, 1, 16, 2 * i - 8, 2 * lax.axis_size("gx"))
    for p in (0, 17):
        gain[p] = OMEGA / jnp.maximum(de[p], 0.01)
    op.first_sweep(v2, fe, 0, 17)
    op.sweep(v2, fe, 1, 16)
    op.defect(r2, v2, fe, 2, 15)
    zero = jnp.zeros((16, 128), F32)
    source = [restrict(r2, 2 + 2 * p, 32, 2) for p in range(7)] + [zero]
    perm = [restrict(ke, 2 + 2 * p, 32, 2) * 0.125 for p in range(7)] + [zero]
    store = [restrict(st, 2 + 2 * p, 32, 2) for p in range(7)] + [zero]
    for i, v in enumerate((source, perm, store)):
        msg[pl.ds(16 * i, 16), :] = pack8(v)


def up_kernel(
    own3, left3, right3,
    t2x, t2y, t2z, s2, g2, v2, r2,
    t1x, t1y, t1z, s1, g1, v1, r1,
    t0x, t0y, t0z, s0, g0, v0, r0, r0h,
    from_left, from_right,
    pressure, residual,
    k3, f3, s3, t3x, t3y, t3z, g3, v3, c2, c1, e1, q1, c0, q0,
):
    n = 0
    for ref in (left3, own3, right3):
        parts = [unpack8(ref[pl.ds(16 * i, 16), :]) for i in range(3)]
        for b in range(7):
            f3[n], k3[n], s3[n] = parts[0][b], parts[1][b], parts[2][b]
            n += 1
    op = Level(3, True, t3x, t3y, t3z, s3, g3)
    op.build(k3, 1, 19, lax.axis_index("gx") - 10, lax.axis_size("gx"))
    op.first_sweep(v3, f3, 1, 19)
    for m in range(1, COARSE):
        op.sweep(v3, f3, 1 + m, 19 - m)
    op = Level(2, True, t2x, t2y, t2z, s2, g2)
    for p in range(5):
        e = v3[8 + p]
        doubled(c2, 4 + 2 * p, e)
        doubled(c2, 5 + 2 * p, e)
    op.sweep(c2, r2, 5, 12)
    op.sweep(c2, r2, 6, 11)
    for p in range(6):
        e = v2[6 + p] + c2[6 + p]
        doubled(c1, 2 * p, e)
        doubled(c1, 2 * p + 1, e)
    for p in range(3, 9):
        q1[p] = r1[p]
    q1[1], q1[2] = unpack2(from_left[pl.ds(64, 64), :])
    q1[9], q1[10] = unpack2(from_right[pl.ds(64, 64), :])
    op = Level(1, True, t1x, t1y, t1z, s1, g1)
    op.sweep(c1, q1, 1, 10)
    op.sweep(c1, q1, 2, 9)
    zero = jnp.zeros((8, 128), F32)
    sub = rows(zero)
    j = lax.axis_index("gy")
    for p in range(8):
        e1[p, pl.ds(0, 8), :] = zero
        e1[p, pl.ds(8, 64), :] = v1[2 + p] + c1[2 + p]
        e1[p, pl.ds(72, 8), :] = zero
    for p in range(8):
        e = e1[p, pl.ds(pl.multiple_of(16 * j, 8), 32), :]
        for q in (2 * p - 1, 2 * p):
            if 0 <= q < 14:
                q0[0, pl.ds(0, 32, stride=2), :] = e
                q0[0, pl.ds(1, 32, stride=2), :] = e
                c0[q, pl.ds(0, 32), :] = q0[0, pl.ds(16, 32), :]
                c0[q, pl.ds(32, 8), :] = jnp.where(
                    sub < 4, q0[0, pl.ds(48, 8), :], q0[0, pl.ds(8, 8), :]
                )
    for p in range(8):
        q0[p + 4, pl.ds(0, 32), :] = r0[p]
        q0[p + 4, pl.ds(32, 8), :] = r0h[p]
    for p in range(2):
        q0[p + 2, pl.ds(0, 40), :] = from_left[pl.ds(128 + 40 * p, 40), :]
        q0[p + 12, pl.ds(0, 40), :] = from_right[pl.ds(128 + 40 * p, 40), :]

    class Source:
        def __getitem__(self, p):
            return q0[p + 1, pl.ds(0, 40), :]

    op = Level(0, False, t0x, t0y, t0z, s0, g0)
    op.sweep(c0, Source(), 1, 12)
    op.sweep(c0, Source(), 2, 11)

    def use(p, here, out):
        pressure[p - 3] = v0[p - 3] + here[:32]
        residual[p - 3] = r0[p - 3] - out[:32]

    op.apply(c0, 3, 10, use)


def call(kernel, outs, scratch, args):
    return pl.pallas_call(
        kernel,
        out_shape=[jax.ShapeDtypeStruct(s, F32) for s in outs],
        scratch_shapes=[pltpu.VMEM(s, F32) for s in scratch],
        compiler_params=pltpu.CompilerParams(vmem_limit_bytes=32 * 1024 * 1024),
    )(*args)


def shifted(x, axis, k):
    n = lax.axis_size(axis)
    return lax.ppermute(x, axis, [(i, i + k) for i in range(n) if 0 <= i + k < n])


def turned(x, axis, k):
    n = lax.axis_size(axis)
    return lax.ppermute(x, axis, [(i, (i + k) % n) for i in range(n)])


def body(permeability, storage, source_term):
    k, s, f = permeability, storage, source_term
    xl = shifted(jnp.concatenate([k[5:], f[6:], s[6:]]), "gx", 1)
    xr = shifted(jnp.concatenate([k[:3], f[:2], s[:2]]), "gx", -1)
    up, down = call(rows_kernel, [(14, 8, 128)] * 2, [], (k, f, s, xl, xr))
    below = shifted(up, "gy", 1)
    above = shifted(down, "gy", -1)
    fine = (14, 40, 128)
    r0, v0, t0x, t0y, t0z, s0, g0, msg = call(
        fine_kernel,
        [(8, 32, 128)] * 2 + [fine] * 5 + [(4, 8, 16, 128)],
        [fine] * 4,
        (k, f, s, xl, xr, above, below),
    )
    gc = lax.all_to_all(msg, "gy", 0, 0)
    gl, gr = shifted(gc, "gx", 1), shifted(gc, "gx", -1)
    mid = (12, 64, 128)
    to_left, to_right, r0h, t1x, t1y, t1z, s1, g1, v1, r1 = call(
        middle_kernel,
        [(208, 128)] * 2 + [(8, 8, 128)] + [mid] * 7,
        [mid] * 2 + [(2, 32, 128)],
        (gc, gl, gr, r0),
    )
    from_left, from_right = turned(to_right, "gx", 1), turned(to_left, "gx", -1)
    blocks = jnp.concatenate([from_left[:64], to_left[:64], from_right[:64]])
    bl, br = turned(blocks, "gx", 3), turned(blocks, "gx", -3)
    low = (18, 32, 128)
    msg3, t2x, t2y, t2z, s2, g2, v2, r2 = call(
        coarse_kernel, [(48, 128)] + [low] * 7, [low] * 3, (blocks, bl, br)
    )
    cl, cr = turned(msg3, "gx", 7), turned(msg3, "gx", -7)
    base = (21, 16, 128)
    pressure, residual = call(
        up_kernel,
        [(8, 32, 128)] * 2,
        [base] * 8 + [low, mid, (8, 80, 128), mid, fine, (15, 64, 128)],
        (
            msg3, cl, cr,
            t2x, t2y, t2z, s2, g2, v2, r2,
            t1x, t1y, t1z, s1, g1, v1, r1,
            t0x, t0y, t0z, s0, g0, v0, r0, r0h,
            from_left, from_right,
        ),
    )
    return pressure, residual


def solution(mesh):
    spec = P(("ma", "gx"), "gy", None)
    return jax.shard_map(
        body, mesh=mesh, in_specs=(spec,) * 3, out_specs=(spec,) * 2, check_vma=False
    )
```

```python
import jax
import jax.numpy as jnp
from jax import lax
from jax.experimental import pallas as pl
from jax.experimental.pallas import tpu as pltpu
from jax.sharding import PartitionSpec as P

OMEGA = 0.7
COARSE = 8
F32 = jnp.float32


def lanes(like):
    return lax.broadcasted_iota(jnp.int32, like.shape, 1)


def rows(like):
    return lax.broadcasted_iota(jnp.int32, like.shape, 0)


def roll(v, shift, axis):
    return pltpu.roll(v, shift % v.shape[axis], axis)


def bit(v, b):
    return (lanes(v) & b) == 0


def swap(v, b, axis=1):
    at = rows(v) if axis == 0 else lanes(v)
    return jnp.where((at & b) == 0, roll(v, -b, axis), roll(v, b, axis))


def split(p, b, axis=1):
    at = rows(p) if axis == 0 else lanes(p)
    low = (at & b) == 0
    return jnp.where(low, p, roll(p, b, axis)), jnp.where(low, roll(p, -b, axis), p)


def pack2(a, b):
    return jnp.where(bit(a, 1), a, b)


def pack4(a, b, c, d):
    return jnp.where(bit(a, 2), pack2(a, b), pack2(c, d))


def exchange(a, b, w):
    low = bit(a, w)
    return jnp.where(low, a, roll(b, w, 1)), jnp.where(low, roll(a, -w, 1), b)


def pack_coarse(a, b, c, d):
    even = (rows(a) & 1) == 0
    return jnp.where(bit(a, 4), jnp.where(even, a, b), jnp.where(even, c, d))


def unpack_coarse(p):
    left, right = split(p, 4)
    return split(left, 1, 0) + split(right, 1, 0)


def harmonic(a, b, level):
    return 2.0**level * 2.0 * a * b / jnp.maximum(a + b, 0.01)


class Level:
    def __init__(self, level, tx, ty, tz, store, gain):
        self.level = level
        self.tx, self.ty, self.tz, self.store, self.gain = tx, ty, tz, store, gain
        self.w = 2**level

    def y_low(self, v):
        if self.level < 2:
            return roll(v, 1, 0)
        n = self.level - 1
        t = roll(v, n, 0)
        return jnp.where(rows(v) < n, roll(t, 1, 1), t)

    def y_high(self, v):
        if self.level < 2:
            return roll(v, -1, 0)
        n = self.level - 1
        t = roll(v, -n, 0)
        return jnp.where(rows(v) >= 8 - n, roll(t, -1, 1), t)

    def build(self, perm, first, last, origin=None, extent=None):
        for p in range(first, last + 2):
            face = harmonic(perm[p], perm[p - 1], self.level)
            if origin is not None:
                at = origin + p
                face = face * jnp.where((at == 0) | (at == extent), 0.0, 1.0)
            self.tx[p] = face
        for p in range(first, last + 1):
            k = perm[p]
            ty = harmonic(k, self.y_low(k), self.level)
            if self.level >= 2:
                outer = (rows(k) < self.level - 1) & ((lanes(k) & 3) == 0)
                ty = jnp.where(outer, 0.0, ty)
            tz = jnp.where(lanes(k) < self.w, 0.0, harmonic(k, roll(k, self.w, 1), self.level))
            self.ty[p] = ty
            self.tz[p] = tz
            d = (
                self.store[p] + self.tx[p] + self.tx[p + 1] + ty + self.y_high(ty)
                + tz + roll(tz, -self.w, 1)
            )
            self.gain[p] = OMEGA / jnp.maximum(d, 0.01)

    def apply(self, v, first, last, use):
        low = self.tx[first] * (v[first] - v[first - 1])
        for p in range(first, last + 1):
            here = v[p]
            high = self.tx[p + 1] * (v[p + 1] - here)
            fy = self.ty[p] * (here - self.y_low(here))
            fz = self.tz[p] * (here - roll(here, self.w, 1))
            out = (
                self.store[p] * here + (low - high) + (fy - self.y_high(fy))
                + (fz - roll(fz, -self.w, 1))
            )
            use(p, here, out)
            low = high

    def sweep(self, v, source, first, last):
        def use(p, here, out):
            v[p] = here + self.gain[p] * (source[p] - out)

        self.apply(v, first, last, use)

    def first_sweep(self, v, source, first, last):
        for p in range(first, last + 1):
            v[p] = self.gain[p] * source[p]

    def defect(self, r, v, source, first, last):
        def use(p, here, out):
            r[p] = source[p] - out

        self.apply(v, first, last, use)


def restrict(ref, p, count, level):
    half = count // 2
    t = ref[p, pl.ds(0, half, stride=2), :] + ref[p, pl.ds(1, half, stride=2), :]
    t = t + (ref[p + 1, pl.ds(0, half, stride=2), :] + ref[p + 1, pl.ds(1, half, stride=2), :])
    return t + swap(t, 2**level)


def restrict_packed(ref, p):
    t = ref[p] + ref[p + 1]
    t = t + swap(t, 1, 0)
    return t + swap(t, 4)


def doubled(ref, p, e):
    half = e.shape[0]
    ref[p, pl.ds(0, half, stride=2), :] = e
    ref[p, pl.ds(1, half, stride=2), :] = e


def planes_kernel(k, f, s, to_left, to_right):
    for p in range(8):
        to_left[p] = k[p]
        to_right[p] = k[p]
    for p in range(6):
        to_left[8 + p] = f[p]
        to_left[14 + p] = s[p]
        to_right[8 + p] = f[2 + p]
        to_right[14 + p] = s[2 + p]


def window(own, left, right, at, edge):
    for p in range(edge):
        yield 8 - edge + p, left, at + p
    for p in range(8):
        yield 8 + p, own, p
    for p in range(edge):
        yield 16 + p, right, at + p


def halo_planes(k, f, s, xl, xr):
    return (
        tuple(window(k, xl, xr, 0, 8)),
        tuple(window(f, xl, xr, 8, 6)),
        tuple(window(s, xl, xr, 14, 6)),
    )


def rows_kernel(k, f, s, xl, xr, up, down):
    n = 0
    for planes in halo_planes(k, f, s, xl, xr):
        for _, ref, p in planes:
            up[n] = ref[p, pl.ds(24, 8), :]
            down[n] = ref[p, pl.ds(0, 8), :]
            n += 1


def fine_kernel(
    k, f, s, xl, xr, above, below,
    slot, ve, re, tx, ty, tz, st, gain, t1x, t1y, t1z, s1, g1,
    ke, fe, k1, f1, v1, r1,
):
    n = 0
    for target, planes in zip((ke, fe, st), halo_planes(k, f, s, xl, xr)):
        for at, ref, p in planes:
            target[at, pl.ds(0, 32), :] = ref[p]
            target[at, pl.ds(32, 8), :] = above[n]
            target[at, pl.ds(40, 8), :] = below[n]
            n += 1
    op = Level(0, tx, ty, tz, st, gain)
    op.build(ke, 2, 21)
    op.first_sweep(ve, fe, 2, 21)
    op.sweep(ve, fe, 3, 20)
    op.defect(re, ve, fe, 4, 19)
    for q in range(12):
        k1[q] = restrict(ke, 2 * q, 48, 0) * 0.125
        if 1 <= q < 11:
            s1[q] = restrict(st, 2 * q, 48, 0)
        if 2 <= q < 10:
            f1[q] = restrict(re, 2 * q, 48, 0)
    op = Level(1, t1x, t1y, t1z, s1, g1)
    op.build(k1, 1, 10)
    op.first_sweep(v1, f1, 2, 9)
    op.sweep(v1, f1, 3, 8)
    op.defect(r1, v1, f1, 4, 7)
    source = [restrict(r1, 4 + 2 * p, 16, 1) for p in range(2)]
    perm = [restrict(k1, 4 + 2 * p, 16, 1) * 0.125 for p in range(2)]
    store = [restrict(s1, 4 + 2 * p, 16, 1) for p in range(2)]
    tiles = [pack4(*source, *perm), pack4(*store, *store)]
    for ref in (r1, v1):
        for p in (4, 6):
            t = pack2(ref[p, pl.ds(0, 16), :], ref[p + 1, pl.ds(0, 16), :])
            tiles += [t[:8], t[8:]]
    for peer in range(16):
        for i, t in enumerate(tiles):
            slot[peer, i] = t


def ring_kernel(g, to_next, to_prev):
    for x in range(4):
        t = [g[4 * x + j, 0] for j in range(4)]
        e0, o0 = exchange(t[0], t[1], 1)
        e1, o1 = exchange(t[2], t[3], 1)
        f0, k0 = exchange(e0, e1, 2)
        f1, k1 = exchange(o0, o1, 2)
        t = [g[4 * x + j, 1] for j in range(4)]
        e0, o0 = exchange(t[0], t[1], 1)
        e1, o1 = exchange(t[2], t[3], 1)
        s0 = jnp.where(bit(e0, 2), e0, e1)
        s1 = jnp.where(bit(o0, 2), o0, o1)
        for out in (to_next, to_prev):
            for at, v in ((0, f0), (1, f1), (8, k0), (9, k1), (16, s0), (17, s1)):
                out[at + 2 * x] = v
    j = lax.axis_index("gy")
    for out, x, v in ((to_next, 3, 8), (to_prev, 0, 6)):
        for i, t in enumerate(edge_tiles(v)):
            out[24 + i] = g[4 * x + peer_of(j, t[0]), t[1]]


def peer_of(j, step):
    return jnp.clip(j + step, 0, 3)


def edge_tiles(v):
    out = []
    for t in (2, 4, v):
        out += [(0, t), (0, t + 1), (1, t), (-1, t + 1)]
    return out


def coarse_kernel(prev, own, nxt, msg, tx, ty, tz, st, gain, v2, r2, ke, fe):
    for b, ref in enumerate((prev, own, nxt)):
        for p in range(8):
            fe[8 * b + p] = ref[p]
            ke[8 * b + p] = ref[8 + p]
            st[8 * b + p] = ref[16 + p]
    op = Level(2, tx, ty, tz, st, gain)
    z = lax.axis_index("gx") // 4
    op.build(ke, 1, 22, 8 * z - 8, 2 * lax.axis_size("gx"))
    op.first_sweep(v2, fe, 1, 22)
    op.sweep(v2, fe, 2, 21)
    op.defect(r2, v2, fe, 3, 20)
    for i, (ref, scale) in enumerate(((r2, None), (ke, 0.125), (st, None))):
        cells = [restrict_packed(ref, 4 + 2 * c) for c in range(8)]
        if scale is not None:
            cells = [c * scale for c in cells]
        msg[2 * i] = pack_coarse(*cells[:4])
        msg[2 * i + 1] = pack_coarse(*cells[4:])


def up_kernel(
    own3, left3, right3,
    t2x, t2y, t2z, s2, g2, v2, r2,
    t1x, t1y, t1z, s1, g1,
    t0x, t0y, t0z, s0, g0, v0, r0,
    slots, prev, nxt,
    pressure, residual,
    k3, f3, s3, t3x, t3y, t3z, g3, v3, c2, e2, c1, q1, w1, dup, c0,
):
    n = 0
    for ref in (left3, own3, right3):
        for half in range(2):
            for i, target in enumerate((f3, k3, s3)):
                for c, v in enumerate(unpack_coarse(ref[2 * i + half])):
                    target[n + c] = v
            n += 4
    i = lax.axis_index("gx")
    j = lax.axis_index("gy")
    z, x = i // 4, i % 4
    op = Level(3, t3x, t3y, t3z, s3, g3)
    op.build(k3, 1, 22, 4 * z - 10, lax.axis_size("gx"))
    op.first_sweep(v3, f3, 1, 22)
    for m in range(1, COARSE):
        op.sweep(v3, f3, 1 + m, 22 - m)
    for n in range(8, 16):
        e = v3[n]
        c2[2 * n - 12] = e
        c2[2 * n - 11] = e
    op = Level(2, t2x, t2y, t2z, s2, g2)
    op.sweep(c2, r2, 5, 18)
    op.sweep(c2, r2, 6, 17)
    for p in range(6, 18):
        e2[p] = v2[p] + c2[p]
    sub = rows(jnp.zeros((8, 128), F32))
    for p in range(6):
        e = e2[6 + 2 * x + p]
        part = []
        for step in (0, 1, -1):
            t = jnp.where((lanes(e) & 3) == j + step, e, 0.0)
            t = t + swap(t, 1)
            part.append(t + swap(t, 2))
        for n, t in enumerate(part):
            doubled(dup, n, t)
        halo = jnp.where(sub < 4, dup[1, pl.ds(0, 8), :], dup[2, pl.ds(8, 8), :])
        for q in (2 * p, 2 * p + 1):
            c1[q, pl.ds(0, 16), :] = dup[0]
            c1[q, pl.ds(16, 8), :] = halo

    def pairs(get, count):
        out = []
        for n in range(count):
            a, b, c, d = (get(4 * n + m) for m in range(4))
            out.append(split(jnp.concatenate([a, b, jnp.where(sub < 4, c, d)], axis=0), 1))
        return out

    def beside(step, v, outer):
        at = 4 * jnp.clip(x + step, 0, 3)
        tiles = edge_tiles(v)
        inside = (x + step >= 0) & (x + step < 4)

        def get(n):
            y, t = tiles[n]
            return jnp.where(inside, slots[at + peer_of(j, y), t], outer[24 + n])

        return pairs(get, 3)

    def own(n):
        y, t = (edge_tiles(6) + edge_tiles(8)[8:])[n]
        return slots[4 * x + peer_of(j, y), t]

    (_, a), (b, c), (d, e) = beside(-1, 8, prev)
    q1[1], q1[2], q1[3], w1[2], w1[3] = a, b, c, d, e
    (a, b), (c, _), (d, e) = beside(1, 6, nxt)
    q1[8], q1[9], q1[10], w1[8], w1[9] = a, b, c, d, e
    (a, b), (c, d), (e, f), (g, h) = pairs(own, 4)
    q1[4], q1[5], q1[6], q1[7] = a, b, c, d
    w1[4], w1[5], w1[6], w1[7] = e, f, g, h
    op = Level(1, t1x, t1y, t1z, s1, g1)
    op.sweep(c1, q1, 1, 10)
    op.sweep(c1, q1, 2, 9)
    for q in range(2, 10):
        e = w1[q] + c1[q]
        doubled(c0, 2 * q, e)
        doubled(c0, 2 * q + 1, e)
    op = Level(0, t0x, t0y, t0z, s0, g0)
    op.sweep(c0, r0, 6, 17)
    op.sweep(c0, r0, 7, 16)

    def use(p, here, out):
        pressure[p - 8] = v0[p, pl.ds(0, 32), :] + here[:32]
        residual[p - 8] = r0[p, pl.ds(0, 32), :] - out[:32]

    op.apply(c0, 8, 15, use)


def call(kernel, outs, scratch, args):
    return pl.pallas_call(
        kernel,
        out_shape=[jax.ShapeDtypeStruct(s, F32) for s in outs],
        scratch_shapes=[pltpu.VMEM(s, F32) for s in scratch],
        compiler_params=pltpu.CompilerParams(vmem_limit_bytes=32 * 1024 * 1024),
    )(*args)


def shifted(x, axis, k):
    n = lax.axis_size(axis)
    return lax.ppermute(x, axis, [(i, i + k) for i in range(n) if 0 <= i + k < n])


def turned(x, axis, k):
    n = lax.axis_size(axis)
    return lax.ppermute(x, axis, [(i, (i + k) % n) for i in range(n)])


def body(permeability, storage, source_term):
    k, s, f = permeability, storage, source_term
    to_left, to_right = call(planes_kernel, [(20, 32, 128)] * 2, [], (k, f, s))
    xl = shifted(to_right, "gx", 1)
    xr = shifted(to_left, "gx", -1)
    up, down = call(rows_kernel, [(64, 8, 128)] * 2, [], (k, f, s, xl, xr))
    below = shifted(up, "gy", 1)
    above = shifted(down, "gy", -1)
    fine, mid = (24, 48, 128), (12, 24, 128)
    slot, v0, r0, t0x, t0y, t0z, s0, g0, t1x, t1y, t1z, s1, g1 = call(
        fine_kernel,
        [(16, 10, 8, 128)] + [fine] * 7 + [mid] * 5,
        [fine] * 2 + [mid] * 4,
        (k, f, s, xl, xr, above, below),
    )
    n = lax.axis_size("gx") * lax.axis_size("gy")
    groups = [[16 * a + b for b in range(16)] for a in range(n // 16)]
    slots = lax.all_to_all(slot, ("gx", "gy"), 0, 0, axis_index_groups=groups)
    to_next, to_prev = call(ring_kernel, [(36, 8, 128)] * 2, [], (slots,))
    prev, nxt = turned(to_next, "gx", 4), turned(to_prev, "gx", -4)
    low = (24, 8, 128)
    msg3, t2x, t2y, t2z, s2, g2, v2, r2 = call(
        coarse_kernel, [(6, 8, 128)] + [low] * 7, [low] * 2, (prev, to_next, nxt)
    )
    left3, right3 = turned(msg3, "gx", 8), turned(msg3, "gx", -8)
    return tuple(call(
        up_kernel,
        [(8, 32, 128)] * 2,
        [low] * 10 + [mid] * 3 + [(3, 16, 128), fine],
        (
            msg3, left3, right3,
            t2x, t2y, t2z, s2, g2, v2, r2,
            t1x, t1y, t1z, s1, g1,
            t0x, t0y, t0z, s0, g0, v0, r0,
            slots, prev, nxt,
        ),
    ))


def solution(mesh):
    spec = P(("ma", "gx"), "gy", None)
    return jax.shard_map(
        body, mesh=mesh, in_specs=(spec,) * 3, out_specs=(spec,) * 2, check_vma=False
    )
```

```python
import jax
import jax.numpy as jnp
from jax import lax
from jax.experimental import pallas as pl
from jax.experimental.pallas import tpu as pltpu
from jax.sharding import PartitionSpec as P

OMEGA = 0.7
COARSE = 8
F32 = jnp.float32


def lanes(like):
    return lax.broadcasted_iota(jnp.int32, like.shape, 1)


def rows(like):
    return lax.broadcasted_iota(jnp.int32, like.shape, 0)


def roll(v, shift, axis):
    return pltpu.roll(v, shift % v.shape[axis], axis)


def bit(v, b):
    return (lanes(v) & b) == 0


def swap(v, b, axis=1):
    at = rows(v) if axis == 0 else lanes(v)
    return jnp.where((at & b) == 0, roll(v, -b, axis), roll(v, b, axis))


def split(p, b, axis=1):
    at = rows(p) if axis == 0 else lanes(p)
    low = (at & b) == 0
    return jnp.where(low, p, roll(p, b, axis)), jnp.where(low, roll(p, -b, axis), p)


def pack2(a, b):
    return jnp.where(bit(a, 1), a, b)


def pack4(a, b, c, d):
    return jnp.where(bit(a, 2), pack2(a, b), pack2(c, d))


def exchange(a, b, w):
    low = bit(a, w)
    return jnp.where(low, a, roll(b, w, 1)), jnp.where(low, roll(a, -w, 1), b)


def pack_coarse(a, b, c, d):
    even = (rows(a) & 1) == 0
    return jnp.where(bit(a, 4), jnp.where(even, a, b), jnp.where(even, c, d))


def unpack_coarse(p):
    left, right = split(p, 4)
    return split(left, 1, 0) + split(right, 1, 0)


def harmonic(a, b, level):
    return 2.0**level * 2.0 * a * b / jnp.maximum(a + b, 0.01)


class Level:
    def __init__(self, level, tx, ty, tz, tzh, store, gain, tyh=None):
        self.level = level
        self.tx, self.ty, self.tz, self.tzh = tx, ty, tz, tzh
        self.store, self.gain, self.tyh = store, gain, tyh
        self.w = 2**level

    def y_low(self, v):
        if self.level < 2:
            return roll(v, 1, 0)
        n = self.level - 1
        t = roll(v, n, 0)
        return jnp.where(rows(v) < n, roll(t, 1, 1), t)

    def y_high(self, v):
        if self.level < 2:
            return roll(v, -1, 0)
        n = self.level - 1
        t = roll(v, -n, 0)
        return jnp.where(rows(v) >= 8 - n, roll(t, -1, 1), t)

    def build(self, perm, first, last, origin=None, extent=None):
        level, w, n = self.level, self.w, self.level - 1
        for p in range(first, last + 2):
            face = harmonic(perm[p], perm[p - 1], level)
            if origin is not None:
                at = origin + p
                face = face * jnp.where((at == 0) | (at == extent), 0.0, 1.0)
            self.tx[p] = face
        for p in range(first, last + 1):
            k = perm[p]
            ty = harmonic(k, self.y_low(k), level)
            if level < 2:
                tyh = roll(ty, -1, 0)
            else:
                tyh = harmonic(k, self.y_high(k), level)
                ty = jnp.where((rows(k) < n) & ((lanes(k) & 3) == 0), 0.0, ty)
                tyh = jnp.where((rows(k) >= 8 - n) & ((lanes(k) & 3) == 3), 0.0, tyh)
                self.tyh[p] = tyh
            tz = jnp.where(lanes(k) < w, 0.0, harmonic(k, roll(k, w, 1), level))
            tzh = jnp.where(lanes(k) >= 128 - w, 0.0, harmonic(k, roll(k, -w, 1), level))
            self.ty[p], self.tz[p], self.tzh[p] = ty, tz, tzh
            d = self.store[p] + self.tx[p] + self.tx[p + 1] + ty + tyh + tz + tzh
            self.gain[p] = OMEGA / jnp.maximum(d, 0.01)

    def apply(self, v, first, last, use):
        low = self.tx[first] * (v[first] - v[first - 1])
        for p in range(first, last + 1):
            here = v[p]
            high = self.tx[p + 1] * (v[p + 1] - here)
            fy = self.ty[p] * (here - self.y_low(here))
            if self.level < 2:
                y = fy - self.y_high(fy)
            else:
                y = fy + self.tyh[p] * (here - self.y_high(here))
            z = self.tz[p] * (here - roll(here, self.w, 1))
            z = z + self.tzh[p] * (here - roll(here, -self.w, 1))
            use(p, here, self.store[p] * here + (low - high) + y + z)
            low = high

    def sweep(self, v, source, first, last):
        def use(p, here, out):
            v[p] = here + self.gain[p] * (source[p] - out)

        self.apply(v, first, last, use)

    def first_sweep(self, v, source, first, last):
        for p in range(first, last + 1):
            v[p] = self.gain[p] * source[p]

    def defect(self, r, v, source, first, last):
        def use(p, here, out):
            r[p] = source[p] - out

        self.apply(v, first, last, use)


def restrict(ref, p, count, level):
    half = count // 2
    t = ref[p, pl.ds(0, half, stride=2), :] + ref[p, pl.ds(1, half, stride=2), :]
    t = t + (ref[p + 1, pl.ds(0, half, stride=2), :] + ref[p + 1, pl.ds(1, half, stride=2), :])
    return t + swap(t, 2**level)


def restrict_packed(ref, p):
    t = ref[p] + ref[p + 1]
    t = t + swap(t, 1, 0)
    return t + swap(t, 4)


def doubled(ref, p, e):
    half = e.shape[0]
    ref[p, pl.ds(0, half, stride=2), :] = e
    ref[p, pl.ds(1, half, stride=2), :] = e


def planes_kernel(k, f, s, to_left, to_right, kv, fv, sv, sems):
    copies = [
        pltpu.make_async_copy(src.at[pl.ds(4 * h, 4)], dst.at[pl.ds(4 * h, 4)], sems.at[2 * i + h])
        for i, (src, dst) in enumerate(((k, kv), (f, fv), (s, sv)))
        for h in range(2)
    ]
    for c in copies:
        c.start()
    for c in copies:
        c.wait()
    for p in range(8):
        to_left[p] = kv[p]
        to_right[p] = kv[p]
    for p in range(6):
        to_left[8 + p] = fv[p]
        to_left[14 + p] = sv[p]
        to_right[8 + p] = fv[2 + p]
        to_right[14 + p] = sv[2 + p]


def window(own, left, right, at, edge):
    for p in range(edge):
        yield 8 - edge + p, left, at + p
    for p in range(8):
        yield 8 + p, own, p
    for p in range(edge):
        yield 16 + p, right, at + p


def halo_planes(k, f, s, xl, xr):
    return (
        tuple(window(k, xl, xr, 0, 8)),
        tuple(window(f, xl, xr, 8, 6)),
        tuple(window(s, xl, xr, 14, 6)),
    )


def rows_kernel(k, f, s, xl, xr, up, down):
    n = 0
    for planes in halo_planes(k, f, s, xl, xr):
        for _, ref, p in planes:
            up[n] = ref[p, pl.ds(24, 8), :]
            down[n] = ref[p, pl.ds(0, 8), :]
            n += 1


def fine_kernel(
    k, f, s, xl, xr, above, below,
    slot, ve, re, tx, ty, tz, tzh, st, gain, t1x, t1y, t1z, t1h, s1, g1,
    ke, fe, k1, f1, v1, r1,
):
    n = 0
    for target, planes in zip((ke, fe, st), halo_planes(k, f, s, xl, xr)):
        for at, ref, p in planes:
            target[at, pl.ds(0, 32), :] = ref[p]
            target[at, pl.ds(32, 8), :] = above[n]
            target[at, pl.ds(40, 8), :] = below[n]
            n += 1
    op = Level(0, tx, ty, tz, tzh, st, gain)
    op.build(ke, 2, 21)
    op.first_sweep(ve, fe, 2, 21)
    op.sweep(ve, fe, 3, 20)
    op.defect(re, ve, fe, 4, 19)
    for q in range(12):
        k1[q] = restrict(ke, 2 * q, 48, 0) * 0.125
        if 1 <= q < 11:
            s1[q] = restrict(st, 2 * q, 48, 0)
        if 2 <= q < 10:
            f1[q] = restrict(re, 2 * q, 48, 0)
    op = Level(1, t1x, t1y, t1z, t1h, s1, g1)
    op.build(k1, 1, 10)
    op.first_sweep(v1, f1, 2, 9)
    op.sweep(v1, f1, 3, 8)
    op.defect(r1, v1, f1, 4, 7)
    source = [restrict(r1, 4 + 2 * p, 16, 1) for p in range(2)]
    perm = [restrict(k1, 4 + 2 * p, 16, 1) * 0.125 for p in range(2)]
    store = [restrict(s1, 4 + 2 * p, 16, 1) for p in range(2)]
    tiles = [pack4(*source, *perm), pack4(*store, *store)]
    for ref in (r1, v1):
        for p in (4, 6):
            t = pack2(ref[p, pl.ds(0, 16), :], ref[p + 1, pl.ds(0, 16), :])
            tiles += [t[:8], t[8:]]
    for peer in range(16):
        for i, t in enumerate(tiles):
            slot[peer, i] = t


def ring_kernel(g, to_next, to_prev):
    for x in range(4):
        t = [g[4 * x + j, 0] for j in range(4)]
        e0, o0 = exchange(t[0], t[1], 1)
        e1, o1 = exchange(t[2], t[3], 1)
        f0, k0 = exchange(e0, e1, 2)
        f1, k1 = exchange(o0, o1, 2)
        t = [g[4 * x + j, 1] for j in range(4)]
        e0, o0 = exchange(t[0], t[1], 1)
        e1, o1 = exchange(t[2], t[3], 1)
        s0 = jnp.where(bit(e0, 2), e0, e1)
        s1 = jnp.where(bit(o0, 2), o0, o1)
        for out in (to_next, to_prev):
            for at, v in ((0, f0), (1, f1), (8, k0), (9, k1), (16, s0), (17, s1)):
                out[at + 2 * x] = v
    j = lax.axis_index("gy")
    for out, x, v in ((to_next, 3, 8), (to_prev, 0, 6)):
        for i, t in enumerate(edge_tiles(v)):
            out[24 + i] = g[4 * x + peer_of(j, t[0]), t[1]]


def peer_of(j, step):
    return jnp.clip(j + step, 0, 3)


def edge_tiles(v):
    out = []
    for t in (2, 4, v):
        out += [(0, t), (0, t + 1), (1, t), (-1, t + 1)]
    return out


def coarse_kernel(
    prev, own, nxt, msg, tx, ty, tyh, tz, tzh, st, gain, v2, r2, ke, fe
):
    for b, ref in enumerate((prev, own, nxt)):
        for p in range(8):
            fe[8 * b + p] = ref[p]
            ke[8 * b + p] = ref[8 + p]
            st[8 * b + p] = ref[16 + p]
    op = Level(2, tx, ty, tz, tzh, st, gain, tyh)
    z = lax.axis_index("gx") // 4
    op.build(ke, 1, 22, 8 * z - 8, 2 * lax.axis_size("gx"))
    op.first_sweep(v2, fe, 1, 22)
    op.sweep(v2, fe, 2, 21)
    op.defect(r2, v2, fe, 3, 20)
    for i, (ref, scale) in enumerate(((r2, None), (ke, 0.125), (st, None))):
        cells = [restrict_packed(ref, 4 + 2 * c) for c in range(8)]
        if scale is not None:
            cells = [c * scale for c in cells]
        msg[2 * i] = pack_coarse(*cells[:4])
        msg[2 * i + 1] = pack_coarse(*cells[4:])


def up_kernel(
    own3, left3, right3,
    t2x, t2y, t2yh, t2z, t2h, s2, g2, v2, r2,
    t1x, t1y, t1z, t1h, s1, g1,
    t0x, t0y, t0z, t0h, s0, g0, v0, r0,
    slots, prev, nxt,
    pressure, residual,
    k3, f3, s3, t3x, t3y, t3yh, t3z, t3h, g3, v3, c2, e2, c1, q1, w1, dup, c0,
):
    n = 0
    for ref in (left3, own3, right3):
        for half in range(2):
            for i, target in enumerate((f3, k3, s3)):
                for c, v in enumerate(unpack_coarse(ref[2 * i + half])):
                    target[n + c] = v
            n += 4
    i = lax.axis_index("gx")
    j = lax.axis_index("gy")
    z, x = i // 4, i % 4
    op = Level(3, t3x, t3y, t3z, t3h, s3, g3, t3yh)
    op.build(k3, 1, 22, 4 * z - 10, lax.axis_size("gx"))
    op.first_sweep(v3, f3, 1, 22)
    for m in range(1, COARSE):
        op.sweep(v3, f3, 1 + m, 22 - m)
    for n in range(8, 16):
        e = v3[n]
        c2[2 * n - 12] = e
        c2[2 * n - 11] = e
    op = Level(2, t2x, t2y, t2z, t2h, s2, g2, t2yh)
    op.sweep(c2, r2, 5, 18)
    op.sweep(c2, r2, 6, 17)
    for p in range(6, 18):
        e2[p] = v2[p] + c2[p]
    sub = rows(jnp.zeros((8, 128), F32))
    for p in range(6):
        e = e2[6 + 2 * x + p]
        part = []
        for step in (0, 1, -1):
            t = jnp.where((lanes(e) & 3) == j + step, e, 0.0)
            t = t + swap(t, 1)
            part.append(t + swap(t, 2))
        for n, t in enumerate(part):
            doubled(dup, n, t)
        halo = jnp.where(sub < 4, dup[1, pl.ds(0, 8), :], dup[2, pl.ds(8, 8), :])
        for q in (2 * p, 2 * p + 1):
            c1[q, pl.ds(0, 16), :] = dup[0]
            c1[q, pl.ds(16, 8), :] = halo

    def pairs(get, count):
        out = []
        for n in range(count):
            a, b, c, d = (get(4 * n + m) for m in range(4))
            out.append(split(jnp.concatenate([a, b, jnp.where(sub < 4, c, d)], axis=0), 1))
        return out

    def beside(step, v, outer):
        at = 4 * jnp.clip(x + step, 0, 3)
        tiles = edge_tiles(v)
        inside = (x + step >= 0) & (x + step < 4)

        def get(n):
            y, t = tiles[n]
            return jnp.where(inside, slots[at + peer_of(j, y), t], outer[24 + n])

        return pairs(get, 3)

    def own(n):
        y, t = (edge_tiles(6) + edge_tiles(8)[8:])[n]
        return slots[4 * x + peer_of(j, y), t]

    (_, a), (b, c), (d, e) = beside(-1, 8, prev)
    q1[1], q1[2], q1[3], w1[2], w1[3] = a, b, c, d, e
    (a, b), (c, _), (d, e) = beside(1, 6, nxt)
    q1[8], q1[9], q1[10], w1[8], w1[9] = a, b, c, d, e
    (a, b), (c, d), (e, f), (g, h) = pairs(own, 4)
    q1[4], q1[5], q1[6], q1[7] = a, b, c, d
    w1[4], w1[5], w1[6], w1[7] = e, f, g, h
    op = Level(1, t1x, t1y, t1z, t1h, s1, g1)
    op.sweep(c1, q1, 1, 10)
    op.sweep(c1, q1, 2, 9)
    for q in range(2, 10):
        e = w1[q] + c1[q]
        doubled(c0, 2 * q, e)
        doubled(c0, 2 * q + 1, e)
    op = Level(0, t0x, t0y, t0z, t0h, s0, g0)
    op.sweep(c0, r0, 6, 17)
    op.sweep(c0, r0, 7, 16)

    def use(p, here, out):
        pressure[p - 8] = v0[p, pl.ds(0, 32), :] + here[:32]
        residual[p - 8] = r0[p, pl.ds(0, 32), :] - out[:32]

    op.apply(c0, 8, 15, use)


def call(kernel, outs, scratch, args):
    return pl.pallas_call(
        kernel,
        out_shape=[jax.ShapeDtypeStruct(s, F32) for s in outs],
        scratch_shapes=[pltpu.VMEM(s, F32) for s in scratch],
        compiler_params=pltpu.CompilerParams(vmem_limit_bytes=32 * 1024 * 1024),
    )(*args)


def shifted(x, axis, k):
    n = lax.axis_size(axis)
    return lax.ppermute(x, axis, [(i, i + k) for i in range(n) if 0 <= i + k < n])


def turned(x, axis, k):
    n = lax.axis_size(axis)
    return lax.ppermute(x, axis, [(i, (i + k) % n) for i in range(n)])


def body(permeability, storage, source_term):
    k, s, f = permeability, storage, source_term
    to_left, to_right, k, f, s = pl.pallas_call(
        planes_kernel,
        out_shape=[
            jax.ShapeDtypeStruct((n, 32, 128), F32) for n in (20, 20, 8, 8, 8)
        ],
        in_specs=[pl.BlockSpec(memory_space=pl.ANY)] * 3,
        scratch_shapes=[pltpu.SemaphoreType.DMA((6,))],
    )(k, f, s)
    xl = shifted(to_right, "gx", 1)
    xr = shifted(to_left, "gx", -1)
    up, down = call(rows_kernel, [(64, 8, 128)] * 2, [], (k, f, s, xl, xr))
    below = shifted(up, "gy", 1)
    above = shifted(down, "gy", -1)
    fine, mid = (24, 48, 128), (12, 24, 128)
    slot, v0, r0, t0x, t0y, t0z, t0h, s0, g0, t1x, t1y, t1z, t1h, s1, g1 = call(
        fine_kernel,
        [(16, 10, 8, 128)] + [fine] * 8 + [mid] * 6,
        [fine] * 2 + [mid] * 4,
        (k, f, s, xl, xr, above, below),
    )
    n = lax.axis_size("gx") * lax.axis_size("gy")
    groups = [[16 * a + b for b in range(16)] for a in range(n // 16)]
    slots = lax.all_to_all(slot, ("gx", "gy"), 0, 0, axis_index_groups=groups)
    to_next, to_prev = call(ring_kernel, [(36, 8, 128)] * 2, [], (slots,))
    prev, nxt = turned(to_next, "gx", 4), turned(to_prev, "gx", -4)
    low = (24, 8, 128)
    msg3, t2x, t2y, t2yh, t2z, t2h, s2, g2, v2, r2 = call(
        coarse_kernel, [(6, 8, 128)] + [low] * 9, [low] * 2, (prev, to_next, nxt)
    )
    left3, right3 = turned(msg3, "gx", 8), turned(msg3, "gx", -8)
    return tuple(call(
        up_kernel,
        [(8, 32, 128)] * 2,
        [low] * 12 + [mid] * 3 + [(3, 16, 128), fine],
        (
            msg3, left3, right3,
            t2x, t2y, t2yh, t2z, t2h, s2, g2, v2, r2,
            t1x, t1y, t1z, t1h, s1, g1,
            t0x, t0y, t0z, t0h, s0, g0, v0, r0,
            slots, prev, nxt,
        ),
    ))


def solution(mesh):
    spec = P(("ma", "gx"), "gy", None)
    return jax.shard_map(
        body, mesh=mesh, in_specs=(spec,) * 3, out_specs=(spec,) * 2, check_vma=False
    )
```

```python
import jax
import jax.numpy as jnp
from jax import lax
from jax.experimental import pallas as pl
from jax.experimental.pallas import tpu as pltpu
from jax.sharding import PartitionSpec as P

OMEGA = 0.7
COARSE = 8
F32 = jnp.float32
PARAMS = pltpu.CompilerParams(vmem_limit_bytes=32 * 1024 * 1024)


def lanes(like):
    return lax.broadcasted_iota(jnp.int32, like.shape, 1)


def rows(like):
    return lax.broadcasted_iota(jnp.int32, like.shape, 0)


def roll(v, shift, axis):
    return pltpu.roll(v, shift % v.shape[axis], axis)


def bit(v, b):
    return (lanes(v) & b) == 0


def swap(v, b, axis=1):
    at = rows(v) if axis == 0 else lanes(v)
    return jnp.where((at & b) == 0, roll(v, -b, axis), roll(v, b, axis))


def split(p, b, axis=1):
    at = rows(p) if axis == 0 else lanes(p)
    low = (at & b) == 0
    return jnp.where(low, p, roll(p, b, axis)), jnp.where(low, roll(p, -b, axis), p)


def pack2(a, b):
    return jnp.where(bit(a, 1), a, b)


def pack4(a, b, c, d):
    return jnp.where(bit(a, 2), pack2(a, b), pack2(c, d))


def exchange(a, b, w):
    low = bit(a, w)
    return jnp.where(low, a, roll(b, w, 1)), jnp.where(low, roll(a, -w, 1), b)


def pack_coarse(a, b, c, d):
    even = (rows(a) & 1) == 0
    return jnp.where(bit(a, 4), jnp.where(even, a, b), jnp.where(even, c, d))


def unpack_coarse(p):
    left, right = split(p, 4)
    return split(left, 1, 0) + split(right, 1, 0)


def harmonic(a, b, level):
    return 2.0**level * 2.0 * a * b / jnp.maximum(a + b, 0.01)


class Level:
    def __init__(self, level, tx, ty, tz, tzh, store, gain, tyh=None):
        self.level = level
        self.tx, self.ty, self.tz, self.tzh = tx, ty, tz, tzh
        self.store, self.gain, self.tyh = store, gain, tyh
        self.w = 2**level

    def y_low(self, v):
        if self.level < 2:
            return roll(v, 1, 0)
        n = self.level - 1
        t = roll(v, n, 0)
        return jnp.where(rows(v) < n, roll(t, 1, 1), t)

    def y_high(self, v):
        if self.level < 2:
            return roll(v, -1, 0)
        n = self.level - 1
        t = roll(v, -n, 0)
        return jnp.where(rows(v) >= 8 - n, roll(t, -1, 1), t)

    def build(self, perm, first, last, origin=None, extent=None):
        level, w, n = self.level, self.w, self.level - 1
        for p in range(first, last + 2):
            face = harmonic(perm[p], perm[p - 1], level)
            if origin is not None:
                at = origin + p
                face = face * jnp.where((at == 0) | (at == extent), 0.0, 1.0)
            self.tx[p] = face
        for p in range(first, last + 1):
            k = perm[p]
            ty = harmonic(k, self.y_low(k), level)
            if level < 2:
                tyh = roll(ty, -1, 0)
            else:
                tyh = harmonic(k, self.y_high(k), level)
                ty = jnp.where((rows(k) < n) & ((lanes(k) & 3) == 0), 0.0, ty)
                tyh = jnp.where((rows(k) >= 8 - n) & ((lanes(k) & 3) == 3), 0.0, tyh)
                self.tyh[p] = tyh
            tz = jnp.where(lanes(k) < w, 0.0, harmonic(k, roll(k, w, 1), level))
            tzh = jnp.where(lanes(k) >= 128 - w, 0.0, harmonic(k, roll(k, -w, 1), level))
            self.ty[p], self.tz[p], self.tzh[p] = ty, tz, tzh
            d = self.store[p] + self.tx[p] + self.tx[p + 1] + ty + tyh + tz + tzh
            self.gain[p] = OMEGA / jnp.maximum(d, 0.01)

    def apply(self, v, first, last, use):
        low = self.tx[first] * (v[first] - v[first - 1])
        for p in range(first, last + 1):
            here = v[p]
            high = self.tx[p + 1] * (v[p + 1] - here)
            fy = self.ty[p] * (here - self.y_low(here))
            if self.level < 2:
                y = fy - self.y_high(fy)
            else:
                y = fy + self.tyh[p] * (here - self.y_high(here))
            z = self.tz[p] * (here - roll(here, self.w, 1))
            z = z + self.tzh[p] * (here - roll(here, -self.w, 1))
            use(p, here, self.store[p] * here + (low - high) + y + z)
            low = high

    def sweep(self, v, source, first, last):
        def use(p, here, out):
            v[p] = here + self.gain[p] * (source[p] - out)

        self.apply(v, first, last, use)

    def first_sweep(self, v, source, first, last):
        for p in range(first, last + 1):
            v[p] = self.gain[p] * source[p]

    def defect(self, r, v, source, first, last):
        def use(p, here, out):
            r[p] = source[p] - out

        self.apply(v, first, last, use)


def restrict(ref, p, count, level):
    half = count // 2
    t = ref[p, pl.ds(0, half, stride=2), :] + ref[p, pl.ds(1, half, stride=2), :]
    t = t + (ref[p + 1, pl.ds(0, half, stride=2), :] + ref[p + 1, pl.ds(1, half, stride=2), :])
    return t + swap(t, 2**level)


def restrict_packed(ref, p):
    t = ref[p] + ref[p + 1]
    t = t + swap(t, 1, 0)
    return t + swap(t, 4)


def doubled(ref, p, e):
    half = e.shape[0]
    ref[p, pl.ds(0, half, stride=2), :] = e
    ref[p, pl.ds(1, half, stride=2), :] = e


def fine_planes(to_left, to_right, xl, xr):
    out = []
    for at, edge, near in ((0, 8, 7), (8, 6, 6), (14, 6, 6)):
        planes = []
        for p in range(edge):
            planes.append((8 - edge + p, xl, at + p, edge - p <= near))
        for p in range(8):
            if p < edge:
                planes.append((8 + p, to_left, at + p, True))
            else:
                planes.append((8 + p, to_right, at + p - 8 + edge, True))
        for p in range(edge):
            planes.append((16 + p, xr, at + p, p < near))
        out.append(planes)
    return out


def rows_kernel(to_left, to_right, xl, xr, up, down):
    n = 0
    for planes in fine_planes(to_left, to_right, xl, xr):
        for _, ref, p, near in planes:
            if near:
                up[n] = ref[p, pl.ds(24, 8), :]
                down[n] = ref[p, pl.ds(0, 8), :]
                n += 1


def fine_kernel(
    to_left, to_right, xl, xr, above, below,
    slot, ve, re, tx, ty, tz, tzh, st, gain, t1x, t1y, t1z, t1h, s1, g1, f1,
    ke, fe, k1, v1, r1,
):
    n = 0
    zero = jnp.zeros((8, 128), F32)
    sub = rows(zero)
    for target, planes in zip((ke, fe, st), fine_planes(to_left, to_right, xl, xr)):
        for at, ref, p, near in planes:
            target[at, pl.ds(0, 32), :] = ref[p]
            target[at, pl.ds(32, 8), :] = above[n] if near else zero
            target[at, pl.ds(40, 8), :] = below[n] if near else zero
            n += near
    op = Level(0, tx, ty, tz, tzh, st, gain)
    op.build(ke, 2, 21)
    op.first_sweep(ve, fe, 2, 21)
    op.sweep(ve, fe, 3, 20)
    op.defect(re, ve, fe, 4, 19)
    for q in range(12):
        k1[q] = restrict(ke, 2 * q, 48, 0) * 0.125
        if 1 <= q < 11:
            s1[q] = restrict(st, 2 * q, 48, 0)
        if 2 <= q < 10:
            f1[q] = restrict(re, 2 * q, 48, 0)
    op = Level(1, t1x, t1y, t1z, t1h, s1, g1)
    op.build(k1, 1, 10)
    op.first_sweep(v1, f1, 2, 9)
    op.sweep(v1, f1, 3, 8)
    op.defect(r1, v1, f1, 4, 7)
    source = [restrict(r1, 4 + 2 * p, 16, 1) for p in range(2)]
    perm = [restrict(k1, 4 + 2 * p, 16, 1) * 0.125 for p in range(2)]
    store = [restrict(s1, 4 + 2 * p, 16, 1) for p in range(2)]
    tiles = [pack4(*source, *perm), pack4(*store, *store), zero, zero, zero]
    for peer in range(16):
        for i, t in enumerate(tiles):
            slot[peer, i] = t
    j = lax.axis_index("gy")
    x = lax.axis_index("gx") % 4
    after, before = (j + 1) % 4, (j + 3) % 4
    first, last = pl.ds(0, 8), pl.ds(8, 8)
    for step, p, q in ((1, 5, 6), (3, 6, 4)):
        to = 4 * ((x + step) % 4)
        slot[to + j, 2] = pack2(r1[5, first, :], r1[6, first, :])
        slot[to + j, 3] = pack2(r1[5, last, :], r1[6, last, :])
        slot[to + j, 4] = pack2(f1[p, first, :], f1[p, last, :])
        slot[to + after, 2] = pack2(r1[q, last, :], r1[q + 1, last, :])
        slot[to + before, 2] = pack2(r1[q, first, :], r1[q + 1, first, :])
    for n in range(2):
        p = 4 + 2 * n
        r = pack2(r1[p, last, :], r1[p + 1, last, :])
        f = pack2(f1[p, last, :], f1[p + 1, last, :])
        slot[4 * x + after, 2 + n] = jnp.where(sub < 4, roll(f, -4, 0), r)
        r = pack2(r1[p, first, :], r1[p + 1, first, :])
        f = pack2(f1[p, first, :], f1[p + 1, first, :])
        slot[4 * x + before, 2 + n] = jnp.where(sub < 4, r, roll(f, 4, 0))


def ring_kernel(g, to_next, to_prev):
    for x in range(4):
        t = [g[4 * x + j, 0] for j in range(4)]
        e0, o0 = exchange(t[0], t[1], 1)
        e1, o1 = exchange(t[2], t[3], 1)
        f0, k0 = exchange(e0, e1, 2)
        f1, k1 = exchange(o0, o1, 2)
        t = [g[4 * x + j, 1] for j in range(4)]
        e0, o0 = exchange(t[0], t[1], 1)
        e1, o1 = exchange(t[2], t[3], 1)
        s0 = jnp.where(bit(e0, 2), e0, e1)
        s1 = jnp.where(bit(o0, 2), o0, o1)
        for out in (to_next, to_prev):
            for at, v in ((0, f0), (1, f1), (8, k0), (9, k1), (16, s0), (17, s1)):
                out[at + 2 * x] = v
    j = lax.axis_index("gy")
    x = lax.axis_index("gx") % 4
    for out, step in ((to_next, 3), (to_prev, 1)):
        at = 4 * ((x + step) % 4)
        for i in range(3):
            out[24 + i] = g[at + j, 2 + i]
        out[27] = g[at + (j + 1) % 4, 2]
        out[28] = g[at + (j + 3) % 4, 2]


def coarse_kernel(
    prev, own, nxt, msg, tx, ty, tyh, tz, tzh, st, gain, v2, r2, ke, fe
):
    for b, ref in enumerate((prev, own, nxt)):
        for p in range(8):
            fe[8 * b + p] = ref[p]
            ke[8 * b + p] = ref[8 + p]
            st[8 * b + p] = ref[16 + p]
    op = Level(2, tx, ty, tz, tzh, st, gain, tyh)
    z = lax.axis_index("gx") // 4
    op.build(ke, 1, 22, 8 * z - 8, 2 * lax.axis_size("gx"))
    op.first_sweep(v2, fe, 1, 22)
    op.sweep(v2, fe, 2, 21)
    op.defect(r2, v2, fe, 3, 20)
    for i, (ref, scale) in enumerate(((r2, None), (ke, 0.125), (st, None))):
        cells = [restrict_packed(ref, 4 + 2 * c) for c in range(8)]
        if scale is not None:
            cells = [c * scale for c in cells]
        msg[2 * i] = pack_coarse(*cells[:4])
        msg[2 * i + 1] = pack_coarse(*cells[4:])


def halo_kernel(slots, prev, nxt, f1, tx, ty, tz, th, st, gain, v, q1, fe):
    zero = jnp.zeros((8, 128), F32)
    sub = rows(zero)
    j = lax.axis_index("gy")
    x = lax.axis_index("gx") % 4
    after, before = (j + 1) % 4, (j + 3) % 4
    first, last, halo = pl.ds(0, 8), pl.ds(8, 8), pl.ds(16, 8)

    def beside(step, outer):
        at = 4 * jnp.clip(x + step, 0, 3)
        inside = (x + step >= 0) & (x + step < 4)
        tiles = ((j, 2), (j, 3), (j, 4), (after, 2), (before, 2))
        return [
            split(jnp.where(inside, slots[at + y, t], outer[24 + n]), 1)
            for n, (y, t) in enumerate(tiles)
        ]

    left, right = beside(-1, prev), beside(1, nxt)
    ends = []
    for n in range(2):
        ends.append((split(slots[4 * x + after, 2 + n], 1), split(slots[4 * x + before, 2 + n], 1)))
    for q in range(2, 10):
        fe[q] = f1[q]
    for q in range(4, 8):
        a, b = (e[q % 2] for e in ends[(q - 4) // 2])
        fe[q, halo, :] = jnp.where(
            sub == 2, roll(a, -4, 0), jnp.where(sub == 5, roll(b, 4, 0), f1[q, halo, :])
        )
    for q, side in ((1, left), (10, right)):
        fe[q, first, :], fe[q, last, :] = side[2]
        fe[q, halo, :] = zero
    op = Level(1, tx, ty, tz, th, st, gain)
    op.first_sweep(v, fe, 1, 10)
    op.sweep(v, fe, 2, 9)
    op.defect(q1, v, fe, 3, 8)
    for q in range(4, 8):
        a, b = (e[q % 2] for e in ends[(q - 4) // 2])
        near = (sub == 1) | (sub == 2)
        q1[q, halo, :] = jnp.where(
            near, a, jnp.where((sub == 5) | (sub == 6), b, q1[q, halo, :])
        )
    for side, q, edge, corner in ((left, 1, 1, 2), (right, 9, 10, 8)):
        for n in range(2):
            q1[q + n, first, :] = side[0][n]
            q1[q + n, last, :] = side[1][n]
        for n in range(2):
            q1[corner + n, halo, :] = jnp.where(sub < 4, side[3][n], side[4][n])
        q1[edge, halo, :] = zero


def up_kernel(
    own3, left3, right3,
    t2x, t2y, t2yh, t2z, t2h, s2, g2, v2, r2,
    t1x, t1y, t1z, t1h, s1, g1,
    t0x, t0y, t0z, t0h, s0, g0, v0, r0,
    w1, q1,
    pressure, residual,
    k3, f3, s3, t3x, t3y, t3yh, t3z, t3h, g3, v3, c2, e2, c1, dup, c0, pv, rv, sems,
):
    n = 0
    for ref in (left3, own3, right3):
        for half in range(2):
            for i, target in enumerate((f3, k3, s3)):
                for c, v in enumerate(unpack_coarse(ref[2 * i + half])):
                    target[n + c] = v
            n += 4
    i = lax.axis_index("gx")
    j = lax.axis_index("gy")
    z, x = i // 4, i % 4
    op = Level(3, t3x, t3y, t3z, t3h, s3, g3, t3yh)
    op.build(k3, 1, 22, 4 * z - 10, lax.axis_size("gx"))
    op.first_sweep(v3, f3, 1, 22)
    for m in range(1, COARSE):
        op.sweep(v3, f3, 1 + m, 22 - m)
    for n in range(8, 16):
        e = v3[n]
        c2[2 * n - 12] = e
        c2[2 * n - 11] = e
    op = Level(2, t2x, t2y, t2z, t2h, s2, g2, t2yh)
    op.sweep(c2, r2, 5, 18)
    op.sweep(c2, r2, 6, 17)
    for p in range(6, 18):
        e2[p] = v2[p] + c2[p]
    sub = rows(jnp.zeros((8, 128), F32))
    for p in range(6):
        e = e2[6 + 2 * x + p]
        part = []
        for step in (0, 1, -1):
            t = jnp.where((lanes(e) & 3) == j + step, e, 0.0)
            t = t + swap(t, 1)
            part.append(t + swap(t, 2))
        for n, t in enumerate(part):
            doubled(dup, n, t)
        halo = jnp.where(sub < 4, dup[1, pl.ds(0, 8), :], dup[2, pl.ds(8, 8), :])
        for q in (2 * p, 2 * p + 1):
            c1[q, pl.ds(0, 16), :] = dup[0]
            c1[q, pl.ds(16, 8), :] = halo

    op = Level(1, t1x, t1y, t1z, t1h, s1, g1)
    op.sweep(c1, q1, 1, 10)
    op.sweep(c1, q1, 2, 9)
    for q in range(2, 10):
        e = w1[q] + c1[q]
        doubled(c0, 2 * q, e)
        doubled(c0, 2 * q + 1, e)
    op = Level(0, t0x, t0y, t0z, t0h, s0, g0)
    op.sweep(c0, r0, 6, 17)
    op.sweep(c0, r0, 7, 16)

    copies = []

    def use(p, here, out):
        n = p - 8
        pv[n] = v0[p, pl.ds(0, 32), :] + here[:32]
        rv[n] = r0[p, pl.ds(0, 32), :] - out[:32]
        if n % 2 == 1:
            two = pl.ds(n - 1, 2)
            for m, (src, dst) in enumerate(((pv, pressure), (rv, residual))):
                c = pltpu.make_async_copy(src.at[two], dst.at[two], sems.at[n - m])
                c.start()
                copies.append(c)

    op.apply(c0, 8, 15, use)
    for c in copies:
        c.wait()


def call(kernel, outs, scratch, args):
    return pl.pallas_call(
        kernel,
        out_shape=[jax.ShapeDtypeStruct(s, F32) for s in outs],
        scratch_shapes=[pltpu.VMEM(s, F32) for s in scratch],
        compiler_params=PARAMS,
    )(*args)


def shifted(x, axis, k):
    n = lax.axis_size(axis)
    return lax.ppermute(x, axis, [(i, i + k) for i in range(n) if 0 <= i + k < n])


def turned(x, axis, k):
    n = lax.axis_size(axis)
    return lax.ppermute(x, axis, [(i, (i + k) % n) for i in range(n)])


def body(permeability, storage, source_term):
    k, s, f = permeability, storage, source_term
    to_left = jnp.concatenate([k, f[:6], s[:6]])
    to_right = jnp.concatenate([k, f[2:], s[2:]])
    xl = shifted(to_right, "gx", 1)
    xr = shifted(to_left, "gx", -1)
    planes = (to_left, to_right, xl, xr)
    up, down = call(rows_kernel, [(62, 8, 128)] * 2, [], planes)
    below = shifted(up, "gy", 1)
    above = shifted(down, "gy", -1)
    fine, mid = (24, 48, 128), (12, 24, 128)
    slot, v0, r0, t0x, t0y, t0z, t0h, s0, g0, t1x, t1y, t1z, t1h, s1, g1, f1 = call(
        fine_kernel,
        [(16, 5, 8, 128)] + [fine] * 8 + [mid] * 7,
        [fine] * 2 + [mid] * 3,
        planes + (above, below),
    )
    n = lax.axis_size("gx") * lax.axis_size("gy")
    groups = [[16 * a + b for b in range(16)] for a in range(n // 16)]
    slots = lax.all_to_all(slot, ("gx", "gy"), 0, 0, axis_index_groups=groups)
    to_next, to_prev = call(ring_kernel, [(29, 8, 128)] * 2, [], (slots,))
    prev, nxt = turned(to_next, "gx", 4), turned(to_prev, "gx", -4)
    low = (24, 8, 128)
    msg3, t2x, t2y, t2yh, t2z, t2h, s2, g2, v2, r2 = call(
        coarse_kernel, [(6, 8, 128)] + [low] * 9, [low] * 2, (prev, to_next, nxt)
    )
    w1, q1 = call(
        halo_kernel, [mid] * 2, [mid], (slots, prev, nxt, f1, t1x, t1y, t1z, t1h, s1, g1)
    )
    left3, right3 = turned(msg3, "gx", 8), turned(msg3, "gx", -8)
    own = (8, 32, 128)
    scratch = [low] * 12 + [mid, (3, 16, 128), fine, own, own]
    args = (
        msg3, left3, right3,
        t2x, t2y, t2yh, t2z, t2h, s2, g2, v2, r2,
        t1x, t1y, t1z, t1h, s1, g1,
        t0x, t0y, t0z, t0h, s0, g0, v0, r0,
        w1, q1,
    )
    return tuple(pl.pallas_call(
        up_kernel,
        out_shape=[jax.ShapeDtypeStruct(own, F32)] * 2,
        out_specs=[pl.BlockSpec(memory_space=pl.ANY)] * 2,
        scratch_shapes=[pltpu.VMEM(n, F32) for n in scratch] + [pltpu.SemaphoreType.DMA((8,))],
        compiler_params=PARAMS,
    )(*args))


def solution(mesh):
    spec = P(("ma", "gx"), "gy", None)
    return jax.shard_map(
        body, mesh=mesh, in_specs=(spec,) * 3, out_specs=(spec,) * 2, check_vma=False
    )
```

```python
import jax
import jax.numpy as jnp
from jax import lax
from jax.experimental import pallas as pl
from jax.experimental.pallas import tpu as pltpu
from jax.sharding import PartitionSpec as P

OMEGA = 0.7
COARSE = 8
F32 = jnp.float32
PARAMS = pltpu.CompilerParams(vmem_limit_bytes=32 * 1024 * 1024)


def lanes(like):
    return lax.broadcasted_iota(jnp.int32, like.shape, 1)


def rows(like):
    return lax.broadcasted_iota(jnp.int32, like.shape, 0)


def roll(v, shift, axis):
    return pltpu.roll(v, shift % v.shape[axis], axis)


def bit(v, b):
    return (lanes(v) & b) == 0


def swap(v, b, axis=1):
    at = rows(v) if axis == 0 else lanes(v)
    return jnp.where((at & b) == 0, roll(v, -b, axis), roll(v, b, axis))


def split(p, b, axis=1):
    at = rows(p) if axis == 0 else lanes(p)
    low = (at & b) == 0
    return jnp.where(low, p, roll(p, b, axis)), jnp.where(low, roll(p, -b, axis), p)


def pack2(a, b):
    return jnp.where(bit(a, 1), a, b)


def pack4(a, b, c, d):
    return jnp.where(bit(a, 2), pack2(a, b), pack2(c, d))


def exchange(a, b, w):
    low = bit(a, w)
    return jnp.where(low, a, roll(b, w, 1)), jnp.where(low, roll(a, -w, 1), b)


def pack_coarse(a, b, c, d):
    even = (rows(a) & 1) == 0
    return jnp.where(bit(a, 4), jnp.where(even, a, b), jnp.where(even, c, d))


def unpack_coarse(p):
    left, right = split(p, 4)
    return split(left, 1, 0) + split(right, 1, 0)


def harmonic(a, b, level):
    return 2.0**level * 2.0 * a * b / jnp.maximum(a + b, 0.01)


class Level:
    def __init__(self, level, tx, ty, tz, tzh, store, gain, tyh=None):
        self.level = level
        self.tx, self.ty, self.tz, self.tzh = tx, ty, tz, tzh
        self.store, self.gain, self.tyh = store, gain, tyh
        self.w = 2**level

    def y_low(self, v):
        if self.level < 2:
            return roll(v, 1, 0)
        n = self.level - 1
        t = roll(v, n, 0)
        return jnp.where(rows(v) < n, roll(t, 1, 1), t)

    def y_high(self, v):
        if self.level < 2:
            return roll(v, -1, 0)
        n = self.level - 1
        t = roll(v, -n, 0)
        return jnp.where(rows(v) >= 8 - n, roll(t, -1, 1), t)

    def build(self, perm, first, last, origin=None, extent=None):
        level, w, n = self.level, self.w, self.level - 1
        for p in range(first, last + 2):
            face = harmonic(perm[p], perm[p - 1], level)
            if origin is not None:
                at = origin + p
                face = face * jnp.where((at == 0) | (at == extent), 0.0, 1.0)
            self.tx[p] = face
        for p in range(first, last + 1):
            k = perm[p]
            ty = harmonic(k, self.y_low(k), level)
            if level < 2:
                tyh = roll(ty, -1, 0)
            else:
                tyh = harmonic(k, self.y_high(k), level)
                ty = jnp.where((rows(k) < n) & ((lanes(k) & 3) == 0), 0.0, ty)
                tyh = jnp.where((rows(k) >= 8 - n) & ((lanes(k) & 3) == 3), 0.0, tyh)
                self.tyh[p] = tyh
            tz = jnp.where(lanes(k) < w, 0.0, harmonic(k, roll(k, w, 1), level))
            tzh = jnp.where(lanes(k) >= 128 - w, 0.0, harmonic(k, roll(k, -w, 1), level))
            self.ty[p], self.tz[p], self.tzh[p] = ty, tz, tzh
            d = self.store[p] + self.tx[p] + self.tx[p + 1] + ty + tyh + tz + tzh
            self.gain[p] = OMEGA / jnp.maximum(d, 0.01)

    def apply(self, v, first, last, use):
        low = self.tx[first] * (v[first] - v[first - 1])
        for p in range(first, last + 1):
            here = v[p]
            high = self.tx[p + 1] * (v[p + 1] - here)
            fy = self.ty[p] * (here - self.y_low(here))
            if self.level < 2:
                y = fy - self.y_high(fy)
            else:
                y = fy + self.tyh[p] * (here - self.y_high(here))
            z = self.tz[p] * (here - roll(here, self.w, 1))
            z = z + self.tzh[p] * (here - roll(here, -self.w, 1))
            use(p, here, self.store[p] * here + (low - high) + y + z)
            low = high

    def sweep(self, v, source, first, last):
        def use(p, here, out):
            v[p] = here + self.gain[p] * (source[p] - out)

        self.apply(v, first, last, use)

    def first_sweep(self, v, source, first, last):
        for p in range(first, last + 1):
            v[p] = self.gain[p] * source[p]

    def defect(self, r, v, source, first, last):
        def use(p, here, out):
            r[p] = source[p] - out

        self.apply(v, first, last, use)


def restrict(ref, p, count, level):
    half = count // 2
    t = ref[p, pl.ds(0, half, stride=2), :] + ref[p, pl.ds(1, half, stride=2), :]
    t = t + (ref[p + 1, pl.ds(0, half, stride=2), :] + ref[p + 1, pl.ds(1, half, stride=2), :])
    return t + swap(t, 2**level)


def restrict_plane(ref, p, level):
    half = ref.shape[1] // 2
    t = ref[p, pl.ds(0, half, stride=2), :] + ref[p, pl.ds(1, half, stride=2), :]
    return t + swap(t, 2**level)


def restrict_packed(ref, p):
    t = ref[p] + ref[p + 1]
    t = t + swap(t, 1, 0)
    return t + swap(t, 4)


def doubled(ref, p, e):
    half = e.shape[0]
    ref[p, pl.ds(0, half, stride=2), :] = e
    ref[p, pl.ds(1, half, stride=2), :] = e


FINE_ROWS = 10 * 48
MESSAGE_ROWS = FINE_ROWS + 3 * 24


def with_rows(target, refs, above, below, at, first):
    for p in range(8):
        target[first + p, pl.ds(0, 32), :] = refs[p]
        target[first + p, pl.ds(32, 8), :] = above[at + p]
        target[first + p, pl.ds(40, 8), :] = below[at + p]


def own_kernel(
    k, f, s, above, below, to_left, to_right,
    ke, fe, st, ve, re, tx, ty, tz, tzh, gain,
):
    for i, (target, ref) in enumerate(((ke, k), (fe, f), (st, s))):
        with_rows(target, ref, above, below, 8 * i, 0)
    op = Level(0, tx, ty, tz, tzh, st, gain)
    op.build(ke, 1, 6)
    op.first_sweep(ve, fe, 1, 6)
    sides = ((to_left, (0, 1, 2, 3)), (to_right, (7, 6, 5, 4)))

    def put(ref, n, v):
        ref[pl.ds(48 * n, 48), :] = v

    for ref, at in sides:
        for n in range(3):
            put(ref, n, ke[at[n]])
        for n in range(2):
            put(ref, 3 + n, fe[at[n]])
            put(ref, 5 + n, st[at[n]])
        put(ref, 7, ve[at[2]])
    op.sweep(ve, fe, 2, 5)
    for ref, at in sides:
        put(ref, 8, ve[at[2]])
        ve[at[1]] = jnp.zeros((48, 128), F32)
    op.defect(re, ve, fe, 2, 5)
    k1 = [restrict(ke, 2 * q, 48, 0) * 0.125 for q in range(4)]
    s1 = [restrict(st, 2 * q, 48, 0) for q in (1, 2)]
    for ref, at in sides:
        put(ref, 9, re[at[2]])
        far = k1[2:] if at[0] == 0 else k1[:2]
        near, mid, last = (k1[1], s1[0], s1[1]) if at[0] == 0 else (k1[2], s1[1], s1[0])
        share = restrict_plane(re, at[3], 0)
        for n, v in enumerate((pack2(*far), pack2(near, mid), pack2(last, share))):
            ref[pl.ds(FINE_ROWS + 24 * n, 24), :] = v


def fine_kernel(
    k, f, s, above, below, xl, xr,
    slot, ve, re, tx, ty, tz, tzh, st, gain, t1x, t1y, t1z, t1h, s1, g1, f1,
    ke, fe, k1, v1, r1,
):
    zero = jnp.zeros((8, 128), F32)
    sub = rows(zero)
    for i, (target, ref) in enumerate(((ke, k), (fe, f), (st, s))):
        with_rows(target, ref, above, below, 8 * i, 8)
    sides = ((xl, (7, 6, 5)), (xr, (16, 17, 18)))

    def got(ref, n):
        return ref[pl.ds(48 * n, 48), :]

    for ref, at in sides:
        for n in range(3):
            ke[at[n]] = got(ref, n)
        for n in range(2):
            fe[at[n]] = got(ref, 3 + n)
            st[at[n]] = got(ref, 5 + n)
        ve[at[2]] = got(ref, 7)
    op = Level(0, tx, ty, tz, tzh, st, gain)
    op.build(ke, 6, 17)
    op.first_sweep(ve, fe, 6, 17)
    op.sweep(ve, fe, 6, 17)
    for ref, at in sides:
        ve[at[2]] = got(ref, 8)
    op.defect(re, ve, fe, 6, 17)
    re[5] = got(xl, 9) + tx[6] * ve[6]
    re[18] = got(xr, 9) + tx[18] * ve[17]
    for q in range(3, 9):
        k1[q] = restrict(ke, 2 * q, 48, 0) * 0.125
        s1[q] = restrict(st, 2 * q, 48, 0)
        f1[q] = restrict(re, 2 * q, 48, 0)
    for ref, lone, far, k2, s2 in ((xl, 5, (0, 1), 2, 1), (xr, 18, (10, 11), 9, 10)):
        a, b, c = (split(ref[pl.ds(FINE_ROWS + 24 * n, 24), :], 1) for n in range(3))
        k1[far[0]], k1[far[1]] = a
        k1[k2], s1[k2] = b
        s1[s2] = c[0]
        f1[k2] = c[1] + restrict_plane(re, lone, 0)
    op = Level(1, t1x, t1y, t1z, t1h, s1, g1)
    op.build(k1, 1, 10)
    op.first_sweep(v1, f1, 2, 9)
    op.sweep(v1, f1, 3, 8)
    op.defect(r1, v1, f1, 4, 7)
    source = [restrict(r1, 4 + 2 * p, 16, 1) for p in range(2)]
    perm = [restrict(k1, 4 + 2 * p, 16, 1) * 0.125 for p in range(2)]
    store = [restrict(s1, 4 + 2 * p, 16, 1) for p in range(2)]
    tiles = [pack4(*source, *perm), pack4(*store, *store), zero, zero, zero]
    for peer in range(16):
        for i, t in enumerate(tiles):
            slot[peer, i] = t
    j = lax.axis_index("gy")
    x = lax.axis_index("gx") % 4
    after, before = (j + 1) % 4, (j + 3) % 4
    first, last = pl.ds(0, 8), pl.ds(8, 8)
    for step, p, q in ((1, 5, 6), (3, 6, 4)):
        to = 4 * ((x + step) % 4)
        slot[to + j, 2] = pack2(r1[5, first, :], r1[6, first, :])
        slot[to + j, 3] = pack2(r1[5, last, :], r1[6, last, :])
        slot[to + j, 4] = pack2(f1[p, first, :], f1[p, last, :])
        slot[to + after, 2] = pack2(r1[q, last, :], r1[q + 1, last, :])
        slot[to + before, 2] = pack2(r1[q, first, :], r1[q + 1, first, :])
    for n in range(2):
        p = 4 + 2 * n
        r = pack2(r1[p, last, :], r1[p + 1, last, :])
        f = pack2(f1[p, last, :], f1[p + 1, last, :])
        slot[4 * x + after, 2 + n] = jnp.where(sub < 4, roll(f, -4, 0), r)
        r = pack2(r1[p, first, :], r1[p + 1, first, :])
        f = pack2(f1[p, first, :], f1[p + 1, first, :])
        slot[4 * x + before, 2 + n] = jnp.where(sub < 4, r, roll(f, 4, 0))


def ring_kernel(g, to_next, to_prev):
    for x in range(4):
        t = [g[4 * x + j, 0] for j in range(4)]
        e0, o0 = exchange(t[0], t[1], 1)
        e1, o1 = exchange(t[2], t[3], 1)
        f0, k0 = exchange(e0, e1, 2)
        f1, k1 = exchange(o0, o1, 2)
        t = [g[4 * x + j, 1] for j in range(4)]
        e0, o0 = exchange(t[0], t[1], 1)
        e1, o1 = exchange(t[2], t[3], 1)
        s0 = jnp.where(bit(e0, 2), e0, e1)
        s1 = jnp.where(bit(o0, 2), o0, o1)
        for out in (to_next, to_prev):
            for at, v in ((0, f0), (1, f1), (8, k0), (9, k1), (16, s0), (17, s1)):
                out[at + 2 * x] = v
    j = lax.axis_index("gy")
    x = lax.axis_index("gx") % 4
    for out, step in ((to_next, 3), (to_prev, 1)):
        at = 4 * ((x + step) % 4)
        for i in range(3):
            out[24 + i] = g[at + j, 2 + i]
        out[27] = g[at + (j + 1) % 4, 2]
        out[28] = g[at + (j + 3) % 4, 2]


def coarse_kernel(
    prev, own, nxt, msg, tx, ty, tyh, tz, tzh, st, gain, v2, r2, ke, fe
):
    for b, ref in enumerate((prev, own, nxt)):
        for p in range(8):
            fe[8 * b + p] = ref[p]
            ke[8 * b + p] = ref[8 + p]
            st[8 * b + p] = ref[16 + p]
    op = Level(2, tx, ty, tz, tzh, st, gain, tyh)
    z = lax.axis_index("gx") // 4
    op.build(ke, 1, 22, 8 * z - 8, 2 * lax.axis_size("gx"))
    op.first_sweep(v2, fe, 1, 22)
    op.sweep(v2, fe, 2, 21)
    op.defect(r2, v2, fe, 3, 20)
    for i, (ref, scale) in enumerate(((r2, None), (ke, 0.125), (st, None))):
        cells = [restrict_packed(ref, 4 + 2 * c) for c in range(8)]
        if scale is not None:
            cells = [c * scale for c in cells]
        msg[2 * i] = pack_coarse(*cells[:4])
        msg[2 * i + 1] = pack_coarse(*cells[4:])


def halo_kernel(slots, prev, nxt, f1, tx, ty, tz, th, st, gain, v, q1, fe):
    zero = jnp.zeros((8, 128), F32)
    sub = rows(zero)
    j = lax.axis_index("gy")
    x = lax.axis_index("gx") % 4
    after, before = (j + 1) % 4, (j + 3) % 4
    first, last, halo = pl.ds(0, 8), pl.ds(8, 8), pl.ds(16, 8)

    def beside(step, outer):
        at = 4 * jnp.clip(x + step, 0, 3)
        inside = (x + step >= 0) & (x + step < 4)
        tiles = ((j, 2), (j, 3), (j, 4), (after, 2), (before, 2))
        return [
            split(jnp.where(inside, slots[at + y, t], outer[24 + n]), 1)
            for n, (y, t) in enumerate(tiles)
        ]

    left, right = beside(-1, prev), beside(1, nxt)
    ends = []
    for n in range(2):
        ends.append((split(slots[4 * x + after, 2 + n], 1), split(slots[4 * x + before, 2 + n], 1)))
    for q in range(2, 10):
        fe[q] = f1[q]
    for q in range(4, 8):
        a, b = (e[q % 2] for e in ends[(q - 4) // 2])
        fe[q, halo, :] = jnp.where(
            sub == 2, roll(a, -4, 0), jnp.where(sub == 5, roll(b, 4, 0), f1[q, halo, :])
        )
    for q, side in ((1, left), (10, right)):
        fe[q, first, :], fe[q, last, :] = side[2]
        fe[q, halo, :] = zero
    op = Level(1, tx, ty, tz, th, st, gain)
    op.first_sweep(v, fe, 1, 10)
    op.sweep(v, fe, 2, 9)
    op.defect(q1, v, fe, 3, 8)
    for q in range(4, 8):
        a, b = (e[q % 2] for e in ends[(q - 4) // 2])
        near = (sub == 1) | (sub == 2)
        q1[q, halo, :] = jnp.where(
            near, a, jnp.where((sub == 5) | (sub == 6), b, q1[q, halo, :])
        )
    for side, q, edge, corner in ((left, 1, 1, 2), (right, 9, 10, 8)):
        for n in range(2):
            q1[q + n, first, :] = side[0][n]
            q1[q + n, last, :] = side[1][n]
        for n in range(2):
            q1[corner + n, halo, :] = jnp.where(sub < 4, side[3][n], side[4][n])
        q1[edge, halo, :] = zero


def up_kernel(
    own3, left3, right3,
    t2x, t2y, t2yh, t2z, t2h, s2, g2, v2, r2,
    t1x, t1y, t1z, t1h, s1, g1,
    t0x, t0y, t0z, t0h, s0, g0, v0, r0,
    w1, q1,
    pressure, residual,
    k3, f3, s3, t3x, t3y, t3yh, t3z, t3h, g3, v3, c2, e2, c1, dup, c0, pv, rv, sems,
):
    n = 0
    for ref in (left3, own3, right3):
        for half in range(2):
            for i, target in enumerate((f3, k3, s3)):
                for c, v in enumerate(unpack_coarse(ref[2 * i + half])):
                    target[n + c] = v
            n += 4
    i = lax.axis_index("gx")
    j = lax.axis_index("gy")
    z, x = i // 4, i % 4
    op = Level(3, t3x, t3y, t3z, t3h, s3, g3, t3yh)
    op.build(k3, 1, 22, 4 * z - 10, lax.axis_size("gx"))
    op.first_sweep(v3, f3, 1, 22)
    for m in range(1, COARSE):
        op.sweep(v3, f3, 1 + m, 22 - m)
    for n in range(8, 16):
        e = v3[n]
        c2[2 * n - 12] = e
        c2[2 * n - 11] = e
    op = Level(2, t2x, t2y, t2z, t2h, s2, g2, t2yh)
    op.sweep(c2, r2, 5, 18)
    op.sweep(c2, r2, 6, 17)
    for p in range(6, 18):
        e2[p] = v2[p] + c2[p]
    sub = rows(jnp.zeros((8, 128), F32))
    for p in range(6):
        e = e2[6 + 2 * x + p]
        part = []
        for step in (0, 1, -1):
            t = jnp.where((lanes(e) & 3) == j + step, e, 0.0)
            t = t + swap(t, 1)
            part.append(t + swap(t, 2))
        for n, t in enumerate(part):
            doubled(dup, n, t)
        halo = jnp.where(sub < 4, dup[1, pl.ds(0, 8), :], dup[2, pl.ds(8, 8), :])
        for q in (2 * p, 2 * p + 1):
            c1[q, pl.ds(0, 16), :] = dup[0]
            c1[q, pl.ds(16, 8), :] = halo

    op = Level(1, t1x, t1y, t1z, t1h, s1, g1)
    op.sweep(c1, q1, 1, 10)
    op.sweep(c1, q1, 2, 9)
    for q in range(2, 10):
        e = w1[q] + c1[q]
        doubled(c0, 2 * q, e)
        doubled(c0, 2 * q + 1, e)
    op = Level(0, t0x, t0y, t0z, t0h, s0, g0)
    op.sweep(c0, r0, 6, 17)
    op.sweep(c0, r0, 7, 16)

    copies = []

    def use(p, here, out):
        n = p - 8
        pv[n] = v0[p, pl.ds(0, 32), :] + here[:32]
        rv[n] = r0[p, pl.ds(0, 32), :] - out[:32]
        if n % 2 == 1:
            two = pl.ds(n - 1, 2)
            for m, (src, dst) in enumerate(((pv, pressure), (rv, residual))):
                c = pltpu.make_async_copy(src.at[two], dst.at[two], sems.at[n - m])
                c.start()
                copies.append(c)

    op.apply(c0, 8, 15, use)
    for c in copies:
        c.wait()


def call(kernel, outs, scratch, args):
    return pl.pallas_call(
        kernel,
        out_shape=[jax.ShapeDtypeStruct(s, F32) for s in outs],
        scratch_shapes=[pltpu.VMEM(s, F32) for s in scratch],
        compiler_params=PARAMS,
    )(*args)


def shifted(x, axis, k):
    n = lax.axis_size(axis)
    return lax.ppermute(x, axis, [(i, i + k) for i in range(n) if 0 <= i + k < n])


def turned(x, axis, k):
    n = lax.axis_size(axis)
    return lax.ppermute(x, axis, [(i, (i + k) % n) for i in range(n)])


def body(permeability, storage, source_term):
    k, s, f = permeability, storage, source_term
    above = shifted(jnp.concatenate([k[:, :8], f[:, :8], s[:, :8]]), "gy", -1)
    below = shifted(jnp.concatenate([k[:, 24:], f[:, 24:], s[:, 24:]]), "gy", 1)
    own = (k, f, s, above, below)
    to_left, to_right = call(
        own_kernel, [(MESSAGE_ROWS, 128)] * 2, [(8, 48, 128)] * 10, own
    )
    xl, xr = shifted(to_right, "gx", 1), shifted(to_left, "gx", -1)
    fine, mid = (24, 48, 128), (12, 24, 128)
    slot, v0, r0, t0x, t0y, t0z, t0h, s0, g0, t1x, t1y, t1z, t1h, s1, g1, f1 = call(
        fine_kernel,
        [(16, 5, 8, 128)] + [fine] * 8 + [mid] * 7,
        [fine] * 2 + [mid] * 3,
        own + (xl, xr),
    )
    n = lax.axis_size("gx") * lax.axis_size("gy")
    groups = [[16 * a + b for b in range(16)] for a in range(n // 16)]
    slots = lax.all_to_all(slot, ("gx", "gy"), 0, 0, axis_index_groups=groups)
    to_next, to_prev = call(ring_kernel, [(29, 8, 128)] * 2, [], (slots,))
    prev, nxt = turned(to_next, "gx", 4), turned(to_prev, "gx", -4)
    low = (24, 8, 128)
    msg3, t2x, t2y, t2yh, t2z, t2h, s2, g2, v2, r2 = call(
        coarse_kernel, [(6, 8, 128)] + [low] * 9, [low] * 2, (prev, to_next, nxt)
    )
    w1, q1 = call(
        halo_kernel, [mid] * 2, [mid], (slots, prev, nxt, f1, t1x, t1y, t1z, t1h, s1, g1)
    )
    left3, right3 = turned(msg3, "gx", 8), turned(msg3, "gx", -8)
    own = (8, 32, 128)
    scratch = [low] * 12 + [mid, (3, 16, 128), fine, own, own]
    args = (
        msg3, left3, right3,
        t2x, t2y, t2yh, t2z, t2h, s2, g2, v2, r2,
        t1x, t1y, t1z, t1h, s1, g1,
        t0x, t0y, t0z, t0h, s0, g0, v0, r0,
        w1, q1,
    )
    return tuple(pl.pallas_call(
        up_kernel,
        out_shape=[jax.ShapeDtypeStruct(own, F32)] * 2,
        out_specs=[pl.BlockSpec(memory_space=pl.ANY)] * 2,
        scratch_shapes=[pltpu.VMEM(n, F32) for n in scratch] + [pltpu.SemaphoreType.DMA((8,))],
        compiler_params=PARAMS,
    )(*args))


def solution(mesh):
    spec = P(("ma", "gx"), "gy", None)
    return jax.shard_map(
        body, mesh=mesh, in_specs=(spec,) * 3, out_specs=(spec,) * 2, check_vma=False
    )
```

```python
import jax
import jax.numpy as jnp
from jax import lax
from jax.experimental import pallas as pl
from jax.experimental.pallas import tpu as pltpu
from jax.sharding import PartitionSpec as P

OMEGA = 0.7
COARSE = 8
F32 = jnp.float32
PARAMS = pltpu.CompilerParams(vmem_limit_bytes=32 * 1024 * 1024)


def lanes(like):
    return lax.broadcasted_iota(jnp.int32, like.shape, 1)


def rows(like):
    return lax.broadcasted_iota(jnp.int32, like.shape, 0)


def roll(v, shift, axis):
    return pltpu.roll(v, shift % v.shape[axis], axis)


def bit(v, b):
    return (lanes(v) & b) == 0


def swap(v, b, axis=1):
    at = rows(v) if axis == 0 else lanes(v)
    return jnp.where((at & b) == 0, roll(v, -b, axis), roll(v, b, axis))


def split(p, b, axis=1):
    at = rows(p) if axis == 0 else lanes(p)
    low = (at & b) == 0
    return jnp.where(low, p, roll(p, b, axis)), jnp.where(low, roll(p, -b, axis), p)


def pack2(a, b):
    return jnp.where(bit(a, 1), a, b)


def pack4(a, b, c, d):
    return jnp.where(bit(a, 2), pack2(a, b), pack2(c, d))


def exchange(a, b, w):
    low = bit(a, w)
    return jnp.where(low, a, roll(b, w, 1)), jnp.where(low, roll(a, -w, 1), b)


def pack_coarse(a, b, c, d):
    even = (rows(a) & 1) == 0
    return jnp.where(bit(a, 4), jnp.where(even, a, b), jnp.where(even, c, d))


def unpack_coarse(p):
    left, right = split(p, 4)
    return split(left, 1, 0) + split(right, 1, 0)


def harmonic(a, b, level):
    return 2.0**level * 2.0 * a * b / jnp.maximum(a + b, 0.01)


class Level:
    def __init__(self, level, tx, ty, tz, tzh, store, gain, tyh=None):
        self.level = level
        self.tx, self.ty, self.tz, self.tzh = tx, ty, tz, tzh
        self.store, self.gain, self.tyh = store, gain, tyh
        self.w = 2**level

    def y_low(self, v):
        if self.level < 2:
            return roll(v, 1, 0)
        n = self.level - 1
        t = roll(v, n, 0)
        return jnp.where(rows(v) < n, roll(t, 1, 1), t)

    def y_high(self, v):
        if self.level < 2:
            return roll(v, -1, 0)
        n = self.level - 1
        t = roll(v, -n, 0)
        return jnp.where(rows(v) >= 8 - n, roll(t, -1, 1), t)

    def build(self, perm, first, last, origin=None, extent=None):
        level, w, n = self.level, self.w, self.level - 1
        for p in range(first, last + 2):
            face = harmonic(perm[p], perm[p - 1], level)
            if origin is not None:
                at = origin + p
                face = face * jnp.where((at == 0) | (at == extent), 0.0, 1.0)
            self.tx[p] = face
        for p in range(first, last + 1):
            k = perm[p]
            ty = harmonic(k, self.y_low(k), level)
            if level < 2:
                tyh = roll(ty, -1, 0)
            else:
                tyh = harmonic(k, self.y_high(k), level)
                ty = jnp.where((rows(k) < n) & ((lanes(k) & 3) == 0), 0.0, ty)
                tyh = jnp.where((rows(k) >= 8 - n) & ((lanes(k) & 3) == 3), 0.0, tyh)
                self.tyh[p] = tyh
            tz = jnp.where(lanes(k) < w, 0.0, harmonic(k, roll(k, w, 1), level))
            tzh = jnp.where(lanes(k) >= 128 - w, 0.0, harmonic(k, roll(k, -w, 1), level))
            self.ty[p], self.tz[p], self.tzh[p] = ty, tz, tzh
            d = self.store[p] + self.tx[p] + self.tx[p + 1] + ty + tyh + tz + tzh
            self.gain[p] = OMEGA / jnp.maximum(d, 0.01)

    def apply(self, v, first, last, use):
        low = self.tx[first] * (v[first] - v[first - 1])
        for p in range(first, last + 1):
            here = v[p]
            high = self.tx[p + 1] * (v[p + 1] - here)
            fy = self.ty[p] * (here - self.y_low(here))
            if self.level < 2:
                y = fy - self.y_high(fy)
            else:
                y = fy + self.tyh[p] * (here - self.y_high(here))
            z = self.tz[p] * (here - roll(here, self.w, 1))
            z = z + self.tzh[p] * (here - roll(here, -self.w, 1))
            use(p, here, self.store[p] * here + (low - high) + y + z)
            low = high

    def sweep(self, v, source, first, last):
        def use(p, here, out):
            v[p] = here + self.gain[p] * (source[p] - out)

        self.apply(v, first, last, use)

    def first_sweep(self, v, source, first, last):
        for p in range(first, last + 1):
            v[p] = self.gain[p] * source[p]

    def defect(self, r, v, source, first, last):
        def use(p, here, out):
            r[p] = source[p] - out

        self.apply(v, first, last, use)


def restrict(ref, p, count, level):
    half = count // 2
    t = ref[p, pl.ds(0, half, stride=2), :] + ref[p, pl.ds(1, half, stride=2), :]
    t = t + (ref[p + 1, pl.ds(0, half, stride=2), :] + ref[p + 1, pl.ds(1, half, stride=2), :])
    return t + swap(t, 2**level)


def restrict_plane(ref, p, level):
    half = ref.shape[1] // 2
    t = ref[p, pl.ds(0, half, stride=2), :] + ref[p, pl.ds(1, half, stride=2), :]
    return t + swap(t, 2**level)


def restrict_packed(ref, p):
    t = ref[p] + ref[p + 1]
    t = t + swap(t, 1, 0)
    return t + swap(t, 4)


def doubled(ref, p, e):
    half = e.shape[0]
    ref[p, pl.ds(0, half, stride=2), :] = e
    ref[p, pl.ds(1, half, stride=2), :] = e


FINE_ROWS = 10 * 48
MESSAGE_ROWS = FINE_ROWS + 3 * 24


def with_rows(target, refs, above, below, at, first):
    for p in range(8):
        target[first + p, pl.ds(0, 32), :] = refs[p]
        target[first + p, pl.ds(32, 8), :] = above[at + p]
        target[first + p, pl.ds(40, 8), :] = below[at + p]


def own_kernel(
    k, f, s, above, below, to_left, to_right,
    ke, fe, st, ve, re, tx, ty, tz, tzh, gain,
):
    for i, (target, ref) in enumerate(((ke, k), (fe, f), (st, s))):
        with_rows(target, ref, above, below, 8 * i, 0)
    op = Level(0, tx, ty, tz, tzh, st, gain)
    op.build(ke, 1, 6)
    op.first_sweep(ve, fe, 1, 6)
    sides = ((to_left, (0, 1, 2, 3)), (to_right, (7, 6, 5, 4)))

    def put(ref, n, v):
        ref[pl.ds(48 * n, 48), :] = v

    for ref, at in sides:
        for n in range(3):
            put(ref, n, ke[at[n]])
        for n in range(2):
            put(ref, 3 + n, fe[at[n]])
            put(ref, 5 + n, st[at[n]])
        put(ref, 7, ve[at[2]])
    op.sweep(ve, fe, 2, 5)
    for ref, at in sides:
        put(ref, 8, ve[at[2]])
        ve[at[1]] = jnp.zeros((48, 128), F32)
    op.defect(re, ve, fe, 2, 5)
    k1 = [restrict(ke, 2 * q, 48, 0) * 0.125 for q in range(4)]
    s1 = [restrict(st, 2 * q, 48, 0) for q in (1, 2)]
    for ref, at in sides:
        put(ref, 9, re[at[2]])
        far = k1[2:] if at[0] == 0 else k1[:2]
        near, mid, last = (k1[1], s1[0], s1[1]) if at[0] == 0 else (k1[2], s1[1], s1[0])
        share = restrict_plane(re, at[3], 0)
        for n, v in enumerate((pack2(*far), pack2(near, mid), pack2(last, share))):
            ref[pl.ds(FINE_ROWS + 24 * n, 24), :] = v


def fine_kernel(
    k, f, s, above, below, xl, xr,
    slot, ve, re, tx, ty, tz, tzh, st, gain, t1x, t1y, t1z, t1h, s1, g1, f1,
    ke, fe, k1, v1, r1,
):
    zero = jnp.zeros((8, 128), F32)
    sub = rows(zero)
    for i, (target, ref) in enumerate(((ke, k), (fe, f), (st, s))):
        with_rows(target, ref, above, below, 8 * i, 8)
    sides = ((xl, (7, 6, 5)), (xr, (16, 17, 18)))

    def got(ref, n):
        return ref[pl.ds(48 * n, 48), :]

    for ref, at in sides:
        for n in range(3):
            ke[at[n]] = got(ref, n)
        for n in range(2):
            fe[at[n]] = got(ref, 3 + n)
            st[at[n]] = got(ref, 5 + n)
        ve[at[2]] = got(ref, 7)
    op = Level(0, tx, ty, tz, tzh, st, gain)
    op.build(ke, 6, 17)
    op.first_sweep(ve, fe, 6, 17)
    op.sweep(ve, fe, 6, 17)
    for ref, at in sides:
        ve[at[2]] = got(ref, 8)
    op.defect(re, ve, fe, 6, 17)
    re[5] = got(xl, 9) + tx[6] * ve[6]
    re[18] = got(xr, 9) + tx[18] * ve[17]
    for q in range(3, 9):
        k1[q] = restrict(ke, 2 * q, 48, 0) * 0.125
        s1[q] = restrict(st, 2 * q, 48, 0)
        f1[q] = restrict(re, 2 * q, 48, 0)
    for ref, lone, far, k2, s2 in ((xl, 5, (0, 1), 2, 1), (xr, 18, (10, 11), 9, 10)):
        a, b, c = (split(ref[pl.ds(FINE_ROWS + 24 * n, 24), :], 1) for n in range(3))
        k1[far[0]], k1[far[1]] = a
        k1[k2], s1[k2] = b
        s1[s2] = c[0]
        f1[k2] = c[1] + restrict_plane(re, lone, 0)
    op = Level(1, t1x, t1y, t1z, t1h, s1, g1)
    op.build(k1, 1, 10)
    op.first_sweep(v1, f1, 2, 9)
    op.sweep(v1, f1, 3, 8)
    op.defect(r1, v1, f1, 4, 7)
    source = [restrict(r1, 4 + 2 * p, 16, 1) for p in range(2)]
    perm = [restrict(k1, 4 + 2 * p, 16, 1) * 0.125 for p in range(2)]
    store = [restrict(s1, 4 + 2 * p, 16, 1) for p in range(2)]
    tiles = [pack4(*source, *perm), pack4(*store, *store), zero, zero, zero]
    for peer in range(16):
        for i, t in enumerate(tiles):
            slot[peer, i] = t
    j = lax.axis_index("gy")
    x = lax.axis_index("gx") % 4
    after, before = (j + 1) % 4, (j + 3) % 4
    first, last = pl.ds(0, 8), pl.ds(8, 8)
    for step, p, q in ((1, 5, 6), (3, 6, 4)):
        to = 4 * ((x + step) % 4)
        slot[to + j, 2] = pack2(r1[5, first, :], r1[6, first, :])
        slot[to + j, 3] = pack2(r1[5, last, :], r1[6, last, :])
        slot[to + j, 4] = pack2(f1[p, first, :], f1[p, last, :])
        slot[to + after, 2] = pack2(r1[q, last, :], r1[q + 1, last, :])
        slot[to + before, 2] = pack2(r1[q, first, :], r1[q + 1, first, :])
    for n in range(2):
        p = 4 + 2 * n
        r = pack2(r1[p, last, :], r1[p + 1, last, :])
        f = pack2(f1[p, last, :], f1[p + 1, last, :])
        slot[4 * x + after, 2 + n] = jnp.where(sub < 4, roll(f, -4, 0), r)
        r = pack2(r1[p, first, :], r1[p + 1, first, :])
        f = pack2(f1[p, first, :], f1[p + 1, first, :])
        slot[4 * x + before, 2 + n] = jnp.where(sub < 4, r, roll(f, 4, 0))


EDGE = 19
TO_NEXT = ((2, 6), (1, 7), (2, 6))
TO_PREV = ((0, 6), (0, 7), (0, 6))


def ring_kernel(g, own, to_next, to_prev):
    for x in range(4):
        t = [g[4 * x + j, 0] for j in range(4)]
        e0, o0 = exchange(t[0], t[1], 1)
        e1, o1 = exchange(t[2], t[3], 1)
        f0, k0 = exchange(e0, e1, 2)
        f1, k1 = exchange(o0, o1, 2)
        t = [g[4 * x + j, 1] for j in range(4)]
        e0, o0 = exchange(t[0], t[1], 1)
        e1, o1 = exchange(t[2], t[3], 1)
        s0 = jnp.where(bit(e0, 2), e0, e1)
        s1 = jnp.where(bit(o0, 2), o0, o1)
        for at, v in ((0, f0), (1, f1), (8, k0), (9, k1), (16, s0), (17, s1)):
            own[at + 2 * x] = v
    for out, parts in ((to_next, TO_NEXT), (to_prev, TO_PREV)):
        n = 0
        for i, (first, count) in enumerate(parts):
            for p in range(first, first + count):
                out[n] = own[8 * i + p]
                n += 1
    j = lax.axis_index("gy")
    x = lax.axis_index("gx") % 4
    for out, step in ((to_next, 3), (to_prev, 1)):
        at = 4 * ((x + step) % 4)
        for i in range(3):
            out[EDGE + i] = g[at + j, 2 + i]
        out[EDGE + 3] = g[at + (j + 1) % 4, 2]
        out[EDGE + 4] = g[at + (j + 3) % 4, 2]


def coarse_kernel(
    prev, own, nxt, msg, tx, ty, tyh, tz, tzh, st, gain, v2, r2, ke, fe
):
    whole = ((0, 8),) * 3
    for b, (ref, parts) in enumerate(((prev, TO_NEXT), (own, whole), (nxt, TO_PREV))):
        n = 0
        for target, (first, count) in zip((fe, ke, st), parts):
            for p in range(first, first + count):
                target[8 * b + p] = ref[n]
                n += 1
    op = Level(2, tx, ty, tz, tzh, st, gain, tyh)
    z = lax.axis_index("gx") // 4
    op.build(ke, 2, 21, 8 * z - 8, 2 * lax.axis_size("gx"))
    op.first_sweep(v2, fe, 2, 21)
    op.sweep(v2, fe, 3, 20)
    op.defect(r2, v2, fe, 4, 19)
    for i, (ref, scale) in enumerate(((r2, None), (ke, 0.125), (st, None))):
        cells = [restrict_packed(ref, 4 + 2 * c) for c in range(8)]
        if scale is not None:
            cells = [c * scale for c in cells]
        msg[2 * i] = pack_coarse(*cells[:4])
        msg[2 * i + 1] = pack_coarse(*cells[4:])


def halo_kernel(slots, prev, nxt, f1, tx, ty, tz, th, st, gain, v, q1, fe):
    zero = jnp.zeros((8, 128), F32)
    sub = rows(zero)
    j = lax.axis_index("gy")
    x = lax.axis_index("gx") % 4
    after, before = (j + 1) % 4, (j + 3) % 4
    first, last, halo = pl.ds(0, 8), pl.ds(8, 8), pl.ds(16, 8)

    def beside(step, outer):
        at = 4 * jnp.clip(x + step, 0, 3)
        inside = (x + step >= 0) & (x + step < 4)
        tiles = ((j, 2), (j, 3), (j, 4), (after, 2), (before, 2))
        return [
            split(jnp.where(inside, slots[at + y, t], outer[EDGE + n]), 1)
            for n, (y, t) in enumerate(tiles)
        ]

    left, right = beside(-1, prev), beside(1, nxt)
    ends = []
    for n in range(2):
        ends.append((split(slots[4 * x + after, 2 + n], 1), split(slots[4 * x + before, 2 + n], 1)))
    for q in range(2, 10):
        fe[q] = f1[q]
    for q in range(4, 8):
        a, b = (e[q % 2] for e in ends[(q - 4) // 2])
        fe[q, halo, :] = jnp.where(
            sub == 2, roll(a, -4, 0), jnp.where(sub == 5, roll(b, 4, 0), f1[q, halo, :])
        )
    for q, side in ((1, left), (10, right)):
        fe[q, first, :], fe[q, last, :] = side[2]
        fe[q, halo, :] = zero
    op = Level(1, tx, ty, tz, th, st, gain)
    op.first_sweep(v, fe, 1, 10)
    op.sweep(v, fe, 2, 9)
    op.defect(q1, v, fe, 3, 8)
    for q in range(4, 8):
        a, b = (e[q % 2] for e in ends[(q - 4) // 2])
        near = (sub == 1) | (sub == 2)
        q1[q, halo, :] = jnp.where(
            near, a, jnp.where((sub == 5) | (sub == 6), b, q1[q, halo, :])
        )
    for side, q, edge, corner in ((left, 1, 1, 2), (right, 9, 10, 8)):
        for n in range(2):
            q1[q + n, first, :] = side[0][n]
            q1[q + n, last, :] = side[1][n]
        for n in range(2):
            q1[corner + n, halo, :] = jnp.where(sub < 4, side[3][n], side[4][n])
        q1[edge, halo, :] = zero


def up_kernel(
    own3, left3, right3,
    t2x, t2y, t2yh, t2z, t2h, s2, g2, v2, r2,
    t1x, t1y, t1z, t1h, s1, g1,
    t0x, t0y, t0z, t0h, s0, g0, v0, r0,
    w1, q1,
    pressure, residual,
    k3, f3, s3, t3x, t3y, t3yh, t3z, t3h, g3, v3, c2, e2, c1, dup, c0, pv, rv, sems,
):
    n = 0
    for ref in (left3, own3, right3):
        for half in range(2):
            for i, target in enumerate((f3, k3, s3)):
                for c, v in enumerate(unpack_coarse(ref[2 * i + half])):
                    target[n + c] = v
            n += 4
    i = lax.axis_index("gx")
    j = lax.axis_index("gy")
    z, x = i // 4, i % 4
    op = Level(3, t3x, t3y, t3z, t3h, s3, g3, t3yh)
    op.build(k3, 1, 22, 4 * z - 10, lax.axis_size("gx"))
    op.first_sweep(v3, f3, 1, 22)
    for m in range(1, COARSE):
        op.sweep(v3, f3, 1 + m, 22 - m)
    for n in range(8, 16):
        e = v3[n]
        c2[2 * n - 12] = e
        c2[2 * n - 11] = e
    op = Level(2, t2x, t2y, t2z, t2h, s2, g2, t2yh)
    op.sweep(c2, r2, 5, 18)
    op.sweep(c2, r2, 6, 17)
    for p in range(6, 18):
        e2[p] = v2[p] + c2[p]
    sub = rows(jnp.zeros((8, 128), F32))
    for p in range(6):
        e = e2[6 + 2 * x + p]
        part = []
        for step in (0, 1, -1):
            t = jnp.where((lanes(e) & 3) == j + step, e, 0.0)
            t = t + swap(t, 1)
            part.append(t + swap(t, 2))
        for n, t in enumerate(part):
            doubled(dup, n, t)
        halo = jnp.where(sub < 4, dup[1, pl.ds(0, 8), :], dup[2, pl.ds(8, 8), :])
        for q in (2 * p, 2 * p + 1):
            c1[q, pl.ds(0, 16), :] = dup[0]
            c1[q, pl.ds(16, 8), :] = halo

    op = Level(1, t1x, t1y, t1z, t1h, s1, g1)
    op.sweep(c1, q1, 1, 10)
    op.sweep(c1, q1, 2, 9)
    for q in range(2, 10):
        e = w1[q] + c1[q]
        doubled(c0, 2 * q, e)
        doubled(c0, 2 * q + 1, e)
    op = Level(0, t0x, t0y, t0z, t0h, s0, g0)
    op.sweep(c0, r0, 6, 17)
    op.sweep(c0, r0, 7, 16)

    copies = []

    def use(p, here, out):
        n = p - 8
        pv[n] = v0[p, pl.ds(0, 32), :] + here[:32]
        rv[n] = r0[p, pl.ds(0, 32), :] - out[:32]
        if n % 2 == 1:
            two = pl.ds(n - 1, 2)
            for m, (src, dst) in enumerate(((pv, pressure), (rv, residual))):
                c = pltpu.make_async_copy(src.at[two], dst.at[two], sems.at[n - m])
                c.start()
                copies.append(c)

    op.apply(c0, 8, 15, use)
    for c in copies:
        c.wait()


def call(kernel, outs, scratch, args):
    return pl.pallas_call(
        kernel,
        out_shape=[jax.ShapeDtypeStruct(s, F32) for s in outs],
        scratch_shapes=[pltpu.VMEM(s, F32) for s in scratch],
        compiler_params=PARAMS,
    )(*args)


def shifted(x, axis, k):
    n = lax.axis_size(axis)
    return lax.ppermute(x, axis, [(i, i + k) for i in range(n) if 0 <= i + k < n])


def turned(x, axis, k):
    n = lax.axis_size(axis)
    return lax.ppermute(x, axis, [(i, (i + k) % n) for i in range(n)])


def stacked(*parts):
    out = jnp.zeros((sum(p.shape[0] for p in parts),) + parts[0].shape[1:], F32)
    at = 0
    for p in parts:
        out = lax.dynamic_update_slice(out, p, (at, 0, 0))
        at += p.shape[0]
    return out


def body(permeability, storage, source_term):
    k, s, f = permeability, storage, source_term
    above = shifted(stacked(k[:, :8], f[:, :8], s[:, :8]), "gy", -1)
    below = shifted(stacked(k[:, 24:], f[:, 24:], s[:, 24:]), "gy", 1)
    own = (k, f, s, above, below)
    to_left, to_right = call(
        own_kernel, [(MESSAGE_ROWS, 128)] * 2, [(8, 48, 128)] * 10, own
    )
    xl, xr = shifted(to_right, "gx", 1), shifted(to_left, "gx", -1)
    fine, mid = (24, 48, 128), (12, 24, 128)
    slot, v0, r0, t0x, t0y, t0z, t0h, s0, g0, t1x, t1y, t1z, t1h, s1, g1, f1 = call(
        fine_kernel,
        [(16, 5, 8, 128)] + [fine] * 8 + [mid] * 7,
        [fine] * 2 + [mid] * 3,
        own + (xl, xr),
    )
    n = lax.axis_size("gx") * lax.axis_size("gy")
    groups = [[16 * a + b for b in range(16)] for a in range(n // 16)]
    slots = lax.all_to_all(slot, ("gx", "gy"), 0, 0, axis_index_groups=groups)
    ring, to_next, to_prev = call(ring_kernel, [(24, 8, 128)] * 3, [], (slots,))
    prev, nxt = turned(to_next, "gx", 4), turned(to_prev, "gx", -4)
    low = (24, 8, 128)
    msg3, t2x, t2y, t2yh, t2z, t2h, s2, g2, v2, r2 = call(
        coarse_kernel, [(6, 8, 128)] + [low] * 9, [low] * 2, (prev, ring, nxt)
    )
    w1, q1 = call(
        halo_kernel, [mid] * 2, [mid], (slots, prev, nxt, f1, t1x, t1y, t1z, t1h, s1, g1)
    )
    left3, right3 = turned(msg3, "gx", 8), turned(msg3, "gx", -8)
    own = (8, 32, 128)
    scratch = [low] * 12 + [mid, (3, 16, 128), fine, own, own]
    args = (
        msg3, left3, right3,
        t2x, t2y, t2yh, t2z, t2h, s2, g2, v2, r2,
        t1x, t1y, t1z, t1h, s1, g1,
        t0x, t0y, t0z, t0h, s0, g0, v0, r0,
        w1, q1,
    )
    return tuple(pl.pallas_call(
        up_kernel,
        out_shape=[jax.ShapeDtypeStruct(own, F32)] * 2,
        out_specs=[pl.BlockSpec(memory_space=pl.ANY)] * 2,
        scratch_shapes=[pltpu.VMEM(n, F32) for n in scratch] + [pltpu.SemaphoreType.DMA((8,))],
        compiler_params=PARAMS,
    )(*args))


def solution(mesh):
    spec = P(("ma", "gx"), "gy", None)
    return jax.shard_map(
        body, mesh=mesh, in_specs=(spec,) * 3, out_specs=(spec,) * 2, check_vma=False
    )
```

```python
import jax
import jax.numpy as jnp
from jax import lax
from jax.experimental import pallas as pl
from jax.experimental.pallas import tpu as pltpu
from jax.sharding import PartitionSpec as P

OMEGA = 0.7
COARSE = 8
F32 = jnp.float32
PARAMS = pltpu.CompilerParams(vmem_limit_bytes=32 * 1024 * 1024)


def lanes(like):
    return lax.broadcasted_iota(jnp.int32, like.shape, 1)


def rows(like):
    return lax.broadcasted_iota(jnp.int32, like.shape, 0)


def roll(v, shift, axis):
    return pltpu.roll(v, shift % v.shape[axis], axis)


def bit(v, b):
    return (lanes(v) & b) == 0


def swap(v, b, axis=1):
    at = rows(v) if axis == 0 else lanes(v)
    return jnp.where((at & b) == 0, roll(v, -b, axis), roll(v, b, axis))


def split(p, b, axis=1):
    at = rows(p) if axis == 0 else lanes(p)
    low = (at & b) == 0
    return jnp.where(low, p, roll(p, b, axis)), jnp.where(low, roll(p, -b, axis), p)


def pack2(a, b):
    return jnp.where(bit(a, 1), a, b)


def pack4(a, b, c, d):
    return jnp.where(bit(a, 2), pack2(a, b), pack2(c, d))


def exchange(a, b, w):
    low = bit(a, w)
    return jnp.where(low, a, roll(b, w, 1)), jnp.where(low, roll(a, -w, 1), b)


def pack_coarse(a, b, c, d):
    even = (rows(a) & 1) == 0
    return jnp.where(bit(a, 4), jnp.where(even, a, b), jnp.where(even, c, d))


def unpack_coarse(p):
    left, right = split(p, 4)
    return split(left, 1, 0) + split(right, 1, 0)


def harmonic(a, b, level):
    return 2.0**level * 2.0 * a * b / jnp.maximum(a + b, 0.01)


class Level:
    def __init__(self, level, tx, ty, tz, tzh, store, gain, tyh=None):
        self.level = level
        self.tx, self.ty, self.tz, self.tzh = tx, ty, tz, tzh
        self.store, self.gain, self.tyh = store, gain, tyh
        self.w = 2**level

    def y_low(self, v):
        if self.level < 2:
            return roll(v, 1, 0)
        n = self.level - 1
        t = roll(v, n, 0)
        return jnp.where(rows(v) < n, roll(t, 1, 1), t)

    def y_high(self, v):
        if self.level < 2:
            return roll(v, -1, 0)
        n = self.level - 1
        t = roll(v, -n, 0)
        return jnp.where(rows(v) >= 8 - n, roll(t, -1, 1), t)

    def build(self, perm, first, last, origin=None, extent=None):
        level, w, n = self.level, self.w, self.level - 1
        for p in range(first, last + 2):
            face = harmonic(perm[p], perm[p - 1], level)
            if origin is not None:
                at = origin + p
                face = face * jnp.where((at == 0) | (at == extent), 0.0, 1.0)
            self.tx[p] = face
        for p in range(first, last + 1):
            k = perm[p]
            ty = harmonic(k, self.y_low(k), level)
            if level < 2:
                tyh = roll(ty, -1, 0)
            else:
                tyh = harmonic(k, self.y_high(k), level)
                ty = jnp.where((rows(k) < n) & ((lanes(k) & 3) == 0), 0.0, ty)
                tyh = jnp.where((rows(k) >= 8 - n) & ((lanes(k) & 3) == 3), 0.0, tyh)
                self.tyh[p] = tyh
            tz = jnp.where(lanes(k) < w, 0.0, harmonic(k, roll(k, w, 1), level))
            tzh = jnp.where(lanes(k) >= 128 - w, 0.0, harmonic(k, roll(k, -w, 1), level))
            self.ty[p], self.tz[p], self.tzh[p] = ty, tz, tzh
            d = self.store[p] + self.tx[p] + self.tx[p + 1] + ty + tyh + tz + tzh
            self.gain[p] = OMEGA / jnp.maximum(d, 0.01)

    def apply(self, v, first, last, use):
        low = self.tx[first] * (v[first] - v[first - 1])
        for p in range(first, last + 1):
            here = v[p]
            high = self.tx[p + 1] * (v[p + 1] - here)
            fy = self.ty[p] * (here - self.y_low(here))
            if self.level < 2:
                y = fy - self.y_high(fy)
            else:
                y = fy + self.tyh[p] * (here - self.y_high(here))
            z = self.tz[p] * (here - roll(here, self.w, 1))
            z = z + self.tzh[p] * (here - roll(here, -self.w, 1))
            use(p, here, self.store[p] * here + (low - high) + y + z)
            low = high

    def sweep(self, v, source, first, last):
        def use(p, here, out):
            v[p] = here + self.gain[p] * (source[p] - out)

        self.apply(v, first, last, use)

    def first_sweep(self, v, source, first, last):
        for p in range(first, last + 1):
            v[p] = self.gain[p] * source[p]

    def defect(self, r, v, source, first, last):
        def use(p, here, out):
            r[p] = source[p] - out

        self.apply(v, first, last, use)


def restrict(ref, p, count, level):
    half = count // 2
    t = ref[p, pl.ds(0, half, stride=2), :] + ref[p, pl.ds(1, half, stride=2), :]
    t = t + (ref[p + 1, pl.ds(0, half, stride=2), :] + ref[p + 1, pl.ds(1, half, stride=2), :])
    return t + swap(t, 2**level)


def restrict_plane(ref, p, level):
    half = ref.shape[1] // 2
    t = ref[p, pl.ds(0, half, stride=2), :] + ref[p, pl.ds(1, half, stride=2), :]
    return t + swap(t, 2**level)


def restrict_packed(ref, p):
    t = ref[p] + ref[p + 1]
    t = t + swap(t, 1, 0)
    return t + swap(t, 4)


def doubled(ref, p, e):
    half = e.shape[0]
    ref[p, pl.ds(0, half, stride=2), :] = e
    ref[p, pl.ds(1, half, stride=2), :] = e


FINE_ROWS = 10 * 48
MESSAGE_ROWS = FINE_ROWS + 3 * 24


def with_rows(target, refs, above, below, at, first):
    for p in range(8):
        target[first + p, pl.ds(0, 32), :] = refs[p]
        target[first + p, pl.ds(32, 8), :] = above[at + p]
        target[first + p, pl.ds(40, 8), :] = below[at + p]


def own_kernel(
    k, f, s, above, below, to_left, to_right,
    ke, fe, st, ve, re, tx, ty, tz, tzh, gain,
):
    for i, (target, ref) in enumerate(((ke, k), (fe, f), (st, s))):
        with_rows(target, ref, above, below, 8 * i, 0)
    op = Level(0, tx, ty, tz, tzh, st, gain)
    op.build(ke, 1, 6)
    op.first_sweep(ve, fe, 1, 6)
    sides = ((to_left, (0, 1, 2, 3)), (to_right, (7, 6, 5, 4)))

    def put(ref, n, v):
        ref[pl.ds(48 * n, 48), :] = v

    for ref, at in sides:
        for n in range(3):
            put(ref, n, ke[at[n]])
        for n in range(2):
            put(ref, 3 + n, fe[at[n]])
            put(ref, 5 + n, st[at[n]])
        put(ref, 7, ve[at[2]])
    op.sweep(ve, fe, 2, 5)
    for ref, at in sides:
        put(ref, 8, ve[at[2]])
        ve[at[1]] = jnp.zeros((48, 128), F32)
    op.defect(re, ve, fe, 2, 5)
    k1 = [restrict(ke, 2 * q, 48, 0) * 0.125 for q in range(4)]
    s1 = [restrict(st, 2 * q, 48, 0) for q in (1, 2)]
    for ref, at in sides:
        put(ref, 9, re[at[2]])
        far = k1[2:] if at[0] == 0 else k1[:2]
        near, mid, last = (k1[1], s1[0], s1[1]) if at[0] == 0 else (k1[2], s1[1], s1[0])
        share = restrict_plane(re, at[3], 0)
        for n, v in enumerate((pack2(*far), pack2(near, mid), pack2(last, share))):
            ref[pl.ds(FINE_ROWS + 24 * n, 24), :] = v


def fine_kernel(
    k, f, s, above, below, xl, xr,
    slot, ve, re, tx, ty, tz, tzh, st, gain, t1x, t1y, t1z, t1h, s1, g1, f1,
    ke, fe, k1, v1, r1,
):
    zero = jnp.zeros((8, 128), F32)
    sub = rows(zero)
    for i, (target, ref) in enumerate(((ke, k), (fe, f), (st, s))):
        with_rows(target, ref, above, below, 8 * i, 8)
    sides = ((xl, (7, 6, 5)), (xr, (16, 17, 18)))

    def got(ref, n):
        return ref[pl.ds(48 * n, 48), :]

    for ref, at in sides:
        for n in range(3):
            ke[at[n]] = got(ref, n)
        for n in range(2):
            fe[at[n]] = got(ref, 3 + n)
            st[at[n]] = got(ref, 5 + n)
        ve[at[2]] = got(ref, 7)
    op = Level(0, tx, ty, tz, tzh, st, gain)
    op.build(ke, 6, 17)
    op.first_sweep(ve, fe, 6, 17)
    op.sweep(ve, fe, 6, 17)
    for ref, at in sides:
        ve[at[2]] = got(ref, 8)
    op.defect(re, ve, fe, 6, 17)
    re[5] = got(xl, 9) + tx[6] * ve[6]
    re[18] = got(xr, 9) + tx[18] * ve[17]
    for q in range(3, 9):
        k1[q] = restrict(ke, 2 * q, 48, 0) * 0.125
        s1[q] = restrict(st, 2 * q, 48, 0)
        f1[q] = restrict(re, 2 * q, 48, 0)
    for ref, lone, far, k2, s2 in ((xl, 5, (0, 1), 2, 1), (xr, 18, (10, 11), 9, 10)):
        a, b, c = (split(ref[pl.ds(FINE_ROWS + 24 * n, 24), :], 1) for n in range(3))
        k1[far[0]], k1[far[1]] = a
        k1[k2], s1[k2] = b
        s1[s2] = c[0]
        f1[k2] = c[1] + restrict_plane(re, lone, 0)
    op = Level(1, t1x, t1y, t1z, t1h, s1, g1)
    op.build(k1, 1, 10)
    op.first_sweep(v1, f1, 2, 9)
    op.sweep(v1, f1, 3, 8)
    op.defect(r1, v1, f1, 4, 7)
    source = [restrict(r1, 4 + 2 * p, 16, 1) for p in range(2)]
    perm = [restrict(k1, 4 + 2 * p, 16, 1) * 0.125 for p in range(2)]
    store = [restrict(s1, 4 + 2 * p, 16, 1) for p in range(2)]
    tiles = [pack4(*source, *perm), pack4(*store, *store), zero, zero, zero]
    for peer in range(16):
        for i, t in enumerate(tiles):
            slot[peer, i] = t
    j = lax.axis_index("gy")
    x = lax.axis_index("gx") % 4
    after, before = (j + 1) % 4, (j + 3) % 4
    first, last = pl.ds(0, 8), pl.ds(8, 8)
    for step, p, q in ((1, 5, 6), (3, 6, 4)):
        to = 4 * ((x + step) % 4)
        slot[to + j, 2] = pack2(r1[5, first, :], r1[6, first, :])
        slot[to + j, 3] = pack2(r1[5, last, :], r1[6, last, :])
        slot[to + j, 4] = pack2(f1[p, first, :], f1[p, last, :])
        slot[to + after, 2] = pack2(r1[q, last, :], r1[q + 1, last, :])
        slot[to + before, 2] = pack2(r1[q, first, :], r1[q + 1, first, :])
    for n in range(2):
        p = 4 + 2 * n
        r = pack2(r1[p, last, :], r1[p + 1, last, :])
        f = pack2(f1[p, last, :], f1[p + 1, last, :])
        slot[4 * x + after, 2 + n] = jnp.where(sub < 4, roll(f, -4, 0), r)
        r = pack2(r1[p, first, :], r1[p + 1, first, :])
        f = pack2(f1[p, first, :], f1[p + 1, first, :])
        slot[4 * x + before, 2 + n] = jnp.where(sub < 4, r, roll(f, 4, 0))


EDGE = 19
TO_NEXT = ((2, 6), (1, 7), (2, 6))
TO_PREV = ((0, 6), (0, 7), (0, 6))


def ring_kernel(g, own, to_next, to_prev):
    for x in range(4):
        t = [g[4 * x + j, 0] for j in range(4)]
        e0, o0 = exchange(t[0], t[1], 1)
        e1, o1 = exchange(t[2], t[3], 1)
        f0, k0 = exchange(e0, e1, 2)
        f1, k1 = exchange(o0, o1, 2)
        t = [g[4 * x + j, 1] for j in range(4)]
        e0, o0 = exchange(t[0], t[1], 1)
        e1, o1 = exchange(t[2], t[3], 1)
        s0 = jnp.where(bit(e0, 2), e0, e1)
        s1 = jnp.where(bit(o0, 2), o0, o1)
        for at, v in ((0, f0), (1, f1), (8, k0), (9, k1), (16, s0), (17, s1)):
            own[at + 2 * x] = v
    for out, parts in ((to_next, TO_NEXT), (to_prev, TO_PREV)):
        n = 0
        for i, (first, count) in enumerate(parts):
            for p in range(first, first + count):
                out[n] = own[8 * i + p]
                n += 1
    j = lax.axis_index("gy")
    x = lax.axis_index("gx") % 4
    for out, step in ((to_next, 3), (to_prev, 1)):
        at = 4 * ((x + step) % 4)
        for i in range(3):
            out[EDGE + i] = g[at + j, 2 + i]
        out[EDGE + 3] = g[at + (j + 1) % 4, 2]
        out[EDGE + 4] = g[at + (j + 3) % 4, 2]


def coarse_kernel(
    prev, own, nxt, msg, tx, ty, tyh, tz, tzh, st, gain, v2, r2, ke, fe
):
    whole = ((0, 8),) * 3
    for b, (ref, parts) in enumerate(((prev, TO_NEXT), (own, whole), (nxt, TO_PREV))):
        n = 0
        for target, (first, count) in zip((fe, ke, st), parts):
            for p in range(first, first + count):
                target[8 * b + p] = ref[n]
                n += 1
    op = Level(2, tx, ty, tz, tzh, st, gain, tyh)
    z = lax.axis_index("gx") // 4
    op.build(ke, 2, 21, 8 * z - 8, 2 * lax.axis_size("gx"))
    op.first_sweep(v2, fe, 2, 21)
    op.sweep(v2, fe, 3, 20)
    op.defect(r2, v2, fe, 4, 19)
    for i, (ref, scale) in enumerate(((r2, None), (ke, 0.125), (st, None))):
        cells = [restrict_packed(ref, 4 + 2 * c) for c in range(8)]
        if scale is not None:
            cells = [c * scale for c in cells]
        msg[2 * i] = pack_coarse(*cells[:4])
        msg[2 * i + 1] = pack_coarse(*cells[4:])


def halo_kernel(slots, prev, nxt, f1, tx, ty, tz, th, st, gain, v, q1, fe):
    zero = jnp.zeros((8, 128), F32)
    sub = rows(zero)
    j = lax.axis_index("gy")
    x = lax.axis_index("gx") % 4
    after, before = (j + 1) % 4, (j + 3) % 4
    first, last, halo = pl.ds(0, 8), pl.ds(8, 8), pl.ds(16, 8)

    def beside(step, outer):
        at = 4 * jnp.clip(x + step, 0, 3)
        inside = (x + step >= 0) & (x + step < 4)
        tiles = ((j, 2), (j, 3), (j, 4), (after, 2), (before, 2))
        return [
            split(jnp.where(inside, slots[at + y, t], outer[EDGE + n]), 1)
            for n, (y, t) in enumerate(tiles)
        ]

    left, right = beside(-1, prev), beside(1, nxt)
    ends = []
    for n in range(2):
        ends.append((split(slots[4 * x + after, 2 + n], 1), split(slots[4 * x + before, 2 + n], 1)))
    for q in range(2, 10):
        fe[q] = f1[q]
    for q in range(4, 8):
        a, b = (e[q % 2] for e in ends[(q - 4) // 2])
        fe[q, halo, :] = jnp.where(
            sub == 2, roll(a, -4, 0), jnp.where(sub == 5, roll(b, 4, 0), f1[q, halo, :])
        )
    for q, side in ((1, left), (10, right)):
        fe[q, first, :], fe[q, last, :] = side[2]
        fe[q, halo, :] = zero
    op = Level(1, tx, ty, tz, th, st, gain)
    op.first_sweep(v, fe, 1, 10)
    op.sweep(v, fe, 2, 9)
    op.defect(q1, v, fe, 3, 8)
    for q in range(4, 8):
        a, b = (e[q % 2] for e in ends[(q - 4) // 2])
        near = (sub == 1) | (sub == 2)
        q1[q, halo, :] = jnp.where(
            near, a, jnp.where((sub == 5) | (sub == 6), b, q1[q, halo, :])
        )
    for side, q, edge, corner in ((left, 1, 1, 2), (right, 9, 10, 8)):
        for n in range(2):
            q1[q + n, first, :] = side[0][n]
            q1[q + n, last, :] = side[1][n]
        for n in range(2):
            q1[corner + n, halo, :] = jnp.where(sub < 4, side[3][n], side[4][n])
        q1[edge, halo, :] = zero


def up_kernel(
    own3, left3, right3,
    t2x, t2y, t2yh, t2z, t2h, s2, g2, v2, r2,
    t1x, t1y, t1z, t1h, s1, g1,
    t0x, t0y, t0z, t0h, s0, g0, v0, r0,
    w1, q1,
    pressure, residual,
    k3, f3, s3, t3x, t3y, t3yh, t3z, t3h, g3, v3, c2, e2, c1, dup, c0, pv, rv, sems,
):
    n = 0
    for ref in (left3, own3, right3):
        for half in range(2):
            for i, target in enumerate((f3, k3, s3)):
                for c, v in enumerate(unpack_coarse(ref[2 * i + half])):
                    target[n + c] = v
            n += 4
    i = lax.axis_index("gx")
    j = lax.axis_index("gy")
    z, x = i // 4, i % 4
    op = Level(3, t3x, t3y, t3z, t3h, s3, g3, t3yh)
    op.build(k3, 1, 22, 4 * z - 10, lax.axis_size("gx"))
    op.first_sweep(v3, f3, 1, 22)
    for m in range(1, COARSE):
        op.sweep(v3, f3, 1 + m, 22 - m)
    for n in range(8, 16):
        e = v3[n]
        c2[2 * n - 12] = e
        c2[2 * n - 11] = e
    op = Level(2, t2x, t2y, t2z, t2h, s2, g2, t2yh)
    op.sweep(c2, r2, 5, 18)
    op.sweep(c2, r2, 6, 17)
    for p in range(6, 18):
        e2[p] = v2[p] + c2[p]
    sub = rows(jnp.zeros((8, 128), F32))
    for p in range(6):
        e = e2[6 + 2 * x + p]
        part = []
        for step in (0, 1, -1):
            t = jnp.where((lanes(e) & 3) == j + step, e, 0.0)
            t = t + swap(t, 1)
            part.append(t + swap(t, 2))
        for n, t in enumerate(part):
            doubled(dup, n, t)
        halo = jnp.where(sub < 4, dup[1, pl.ds(0, 8), :], dup[2, pl.ds(8, 8), :])
        for q in (2 * p, 2 * p + 1):
            c1[q, pl.ds(0, 16), :] = dup[0]
            c1[q, pl.ds(16, 8), :] = halo

    op = Level(1, t1x, t1y, t1z, t1h, s1, g1)
    op.sweep(c1, q1, 1, 10)
    op.sweep(c1, q1, 2, 9)
    for q in range(2, 10):
        e = w1[q] + c1[q]
        doubled(c0, 2 * q, e)
        doubled(c0, 2 * q + 1, e)
    op = Level(0, t0x, t0y, t0z, t0h, s0, g0)
    op.sweep(c0, r0, 6, 17)
    op.sweep(c0, r0, 7, 16)

    copies = []

    def use(p, here, out):
        n = p - 8
        pv[n] = v0[p, pl.ds(0, 32), :] + here[:32]
        rv[n] = r0[p, pl.ds(0, 32), :] - out[:32]
        if n % 2 == 1:
            two = pl.ds(n - 1, 2)
            for m, (src, dst) in enumerate(((pv, pressure), (rv, residual))):
                c = pltpu.make_async_copy(src.at[two], dst.at[two], sems.at[n - m])
                c.start()
                copies.append(c)

    op.apply(c0, 8, 15, use)
    for c in copies:
        c.wait()


def call(kernel, outs, scratch, args):
    return pl.pallas_call(
        kernel,
        out_shape=[jax.ShapeDtypeStruct(s, F32) for s in outs],
        scratch_shapes=[pltpu.VMEM(s, F32) for s in scratch],
        compiler_params=PARAMS,
    )(*args)


def shifted(x, axis, k):
    n = lax.axis_size(axis)
    return lax.ppermute(x, axis, [(i, i + k) for i in range(n) if 0 <= i + k < n])


def turned(x, axis, k):
    n = lax.axis_size(axis)
    return lax.ppermute(x, axis, [(i, (i + k) % n) for i in range(n)])


def body(permeability, storage, source_term):
    k, s, f = permeability, storage, source_term
    parts = (f[:, :8], s[:, :8], f[:, 24:], s[:, 24:])
    (fa, sa, fb, sb), kk = lax.optimization_barrier((parts, k))
    above = shifted(jnp.concatenate([kk[:, :8], fa, sa]), "gy", -1)
    below = shifted(jnp.concatenate([kk[:, 24:], fb, sb]), "gy", 1)
    own = (kk, f, s, above, below)
    to_left, to_right = call(
        own_kernel, [(MESSAGE_ROWS, 128)] * 2, [(8, 48, 128)] * 10, own
    )
    xl, xr = shifted(to_right, "gx", 1), shifted(to_left, "gx", -1)
    fine, mid = (24, 48, 128), (12, 24, 128)
    slot, v0, r0, t0x, t0y, t0z, t0h, s0, g0, t1x, t1y, t1z, t1h, s1, g1, f1 = call(
        fine_kernel,
        [(16, 5, 8, 128)] + [fine] * 8 + [mid] * 7,
        [fine] * 2 + [mid] * 3,
        own + (xl, xr),
    )
    n = lax.axis_size("gx") * lax.axis_size("gy")
    groups = [[16 * a + b for b in range(16)] for a in range(n // 16)]
    slots = lax.all_to_all(slot, ("gx", "gy"), 0, 0, axis_index_groups=groups)
    ring, to_next, to_prev = call(ring_kernel, [(24, 8, 128)] * 3, [], (slots,))
    prev, nxt = turned(to_next, "gx", 4), turned(to_prev, "gx", -4)
    low = (24, 8, 128)
    msg3, t2x, t2y, t2yh, t2z, t2h, s2, g2, v2, r2 = call(
        coarse_kernel, [(6, 8, 128)] + [low] * 9, [low] * 2, (prev, ring, nxt)
    )
    w1, q1 = call(
        halo_kernel, [mid] * 2, [mid], (slots, prev, nxt, f1, t1x, t1y, t1z, t1h, s1, g1)
    )
    left3, right3 = turned(msg3, "gx", 8), turned(msg3, "gx", -8)
    own = (8, 32, 128)
    scratch = [low] * 12 + [mid, (3, 16, 128), fine, own, own]
    args = (
        msg3, left3, right3,
        t2x, t2y, t2yh, t2z, t2h, s2, g2, v2, r2,
        t1x, t1y, t1z, t1h, s1, g1,
        t0x, t0y, t0z, t0h, s0, g0, v0, r0,
        w1, q1,
    )
    return tuple(pl.pallas_call(
        up_kernel,
        out_shape=[jax.ShapeDtypeStruct(own, F32)] * 2,
        out_specs=[pl.BlockSpec(memory_space=pl.ANY)] * 2,
        scratch_shapes=[pltpu.VMEM(n, F32) for n in scratch] + [pltpu.SemaphoreType.DMA((8,))],
        compiler_params=PARAMS,
    )(*args))


def solution(mesh):
    spec = P(("ma", "gx"), "gy", None)
    return jax.shard_map(
        body, mesh=mesh, in_specs=(spec,) * 3, out_specs=(spec,) * 2, check_vma=False
    )
```

```python
import jax
import jax.numpy as jnp
from jax import lax
from jax.experimental import pallas as pl
from jax.experimental.pallas import tpu as pltpu
from jax.sharding import PartitionSpec as P

OMEGA = 0.7
COARSE = 8
F32 = jnp.float32
PARAMS = pltpu.CompilerParams(vmem_limit_bytes=32 * 1024 * 1024)


def lanes(like):
    return lax.broadcasted_iota(jnp.int32, like.shape, 1)


def rows(like):
    return lax.broadcasted_iota(jnp.int32, like.shape, 0)


def roll(v, shift, axis):
    return pltpu.roll(v, shift % v.shape[axis], axis)


def bit(v, b):
    return (lanes(v) & b) == 0


def swap(v, b, axis=1):
    at = rows(v) if axis == 0 else lanes(v)
    return jnp.where((at & b) == 0, roll(v, -b, axis), roll(v, b, axis))


def split(p, b, axis=1):
    at = rows(p) if axis == 0 else lanes(p)
    low = (at & b) == 0
    return jnp.where(low, p, roll(p, b, axis)), jnp.where(low, roll(p, -b, axis), p)


def pack2(a, b):
    return jnp.where(bit(a, 1), a, b)


def pack4(a, b, c, d):
    return jnp.where(bit(a, 2), pack2(a, b), pack2(c, d))


def exchange(a, b, w):
    low = bit(a, w)
    return jnp.where(low, a, roll(b, w, 1)), jnp.where(low, roll(a, -w, 1), b)


def pack_coarse(a, b, c, d):
    even = (rows(a) & 1) == 0
    return jnp.where(bit(a, 4), jnp.where(even, a, b), jnp.where(even, c, d))


def unpack_coarse(p):
    left, right = split(p, 4)
    return split(left, 1, 0) + split(right, 1, 0)


def harmonic(a, b, level):
    return 2.0**level * 2.0 * a * b / jnp.maximum(a + b, 0.01)


class Level:
    def __init__(self, level, tx, ty, tz, tzh, store, gain, tyh=None):
        self.level = level
        self.tx, self.ty, self.tz, self.tzh = tx, ty, tz, tzh
        self.store, self.gain, self.tyh = store, gain, tyh
        self.w = 2**level

    def y_low(self, v):
        if self.level < 2:
            return roll(v, 1, 0)
        n = self.level - 1
        t = roll(v, n, 0)
        return jnp.where(rows(v) < n, roll(t, 1, 1), t)

    def y_high(self, v):
        if self.level < 2:
            return roll(v, -1, 0)
        n = self.level - 1
        t = roll(v, -n, 0)
        return jnp.where(rows(v) >= 8 - n, roll(t, -1, 1), t)

    def build(self, perm, first, last, origin=None, extent=None):
        level, w, n = self.level, self.w, self.level - 1
        for p in range(first, last + 2):
            face = harmonic(perm[p], perm[p - 1], level)
            if origin is not None:
                at = origin + p
                face = face * jnp.where((at == 0) | (at == extent), 0.0, 1.0)
            self.tx[p] = face
        for p in range(first, last + 1):
            k = perm[p]
            ty = harmonic(k, self.y_low(k), level)
            if level < 2:
                tyh = roll(ty, -1, 0)
            else:
                tyh = harmonic(k, self.y_high(k), level)
                ty = jnp.where((rows(k) < n) & ((lanes(k) & 3) == 0), 0.0, ty)
                tyh = jnp.where((rows(k) >= 8 - n) & ((lanes(k) & 3) == 3), 0.0, tyh)
                self.tyh[p] = tyh
            tz = jnp.where(lanes(k) < w, 0.0, harmonic(k, roll(k, w, 1), level))
            tzh = jnp.where(lanes(k) >= 128 - w, 0.0, harmonic(k, roll(k, -w, 1), level))
            self.ty[p], self.tz[p], self.tzh[p] = ty, tz, tzh
            d = self.store[p] + self.tx[p] + self.tx[p + 1] + ty + tyh + tz + tzh
            self.gain[p] = OMEGA / jnp.maximum(d, 0.01)

    def apply(self, v, first, last, use):
        low = self.tx[first] * (v[first] - v[first - 1])
        for p in range(first, last + 1):
            here = v[p]
            high = self.tx[p + 1] * (v[p + 1] - here)
            fy = self.ty[p] * (here - self.y_low(here))
            if self.level < 2:
                y = fy - self.y_high(fy)
            else:
                y = fy + self.tyh[p] * (here - self.y_high(here))
            z = self.tz[p] * (here - roll(here, self.w, 1))
            z = z + self.tzh[p] * (here - roll(here, -self.w, 1))
            use(p, here, self.store[p] * here + (low - high) + y + z)
            low = high

    def sweep(self, v, source, first, last):
        def use(p, here, out):
            v[p] = here + self.gain[p] * (source[p] - out)

        self.apply(v, first, last, use)

    def first_sweep(self, v, source, first, last):
        for p in range(first, last + 1):
            v[p] = self.gain[p] * source[p]

    def defect(self, r, v, source, first, last):
        def use(p, here, out):
            r[p] = source[p] - out

        self.apply(v, first, last, use)


def restrict(ref, p, count, level):
    half = count // 2
    t = ref[p, pl.ds(0, half, stride=2), :] + ref[p, pl.ds(1, half, stride=2), :]
    t = t + (ref[p + 1, pl.ds(0, half, stride=2), :] + ref[p + 1, pl.ds(1, half, stride=2), :])
    return t + swap(t, 2**level)


def restrict_plane(ref, p, level):
    half = ref.shape[1] // 2
    t = ref[p, pl.ds(0, half, stride=2), :] + ref[p, pl.ds(1, half, stride=2), :]
    return t + swap(t, 2**level)


def restrict_packed(ref, p):
    t = ref[p] + ref[p + 1]
    t = t + swap(t, 1, 0)
    return t + swap(t, 4)


def doubled(ref, p, e):
    half = e.shape[0]
    ref[p, pl.ds(0, half, stride=2), :] = e
    ref[p, pl.ds(1, half, stride=2), :] = e


FINE_ROWS = 8 * 48 + 2 * 40
MESSAGE_ROWS = FINE_ROWS + 3 * 24


def with_rows(target, refs, above, below, at, first):
    for p in range(8):
        target[first + p, pl.ds(0, 32), :] = refs[p]
        target[first + p, pl.ds(32, 8), :] = above[at + p]
        target[first + p, pl.ds(40, 8), :] = below[at + p]


def own_kernel(
    k, f, s, above, below, to_left, to_right,
    ke, fe, st, ve, re, tx, ty, tz, tzh, gain,
):
    for i, (target, ref) in enumerate(((ke, k), (fe, f), (st, s))):
        with_rows(target, ref, above, below, 8 * i, 0)
    op = Level(0, tx, ty, tz, tzh, st, gain)
    op.build(ke, 1, 6)
    op.first_sweep(ve, fe, 1, 6)
    sides = ((to_left, (0, 1, 2, 3)), (to_right, (7, 6, 5, 4)))

    def put(ref, n, v):
        ref[pl.ds(48 * n, 48), :] = v

    def put_near(ref, n, v):
        at = 8 * 48 + 40 * n
        ref[pl.ds(at, 32), :] = v[:32]
        ref[pl.ds(at + 32, 8), :] = jnp.where(rows(v[:8]) < 4, v[32:40], v[40:])

    for ref, at in sides:
        for n in range(3):
            put(ref, n, ke[at[n]])
        for n in range(2):
            put(ref, 3 + n, fe[at[n]])
            put(ref, 5 + n, st[at[n]])
        put(ref, 7, ve[at[2]])
    op.sweep(ve, fe, 2, 5)
    for ref, at in sides:
        put_near(ref, 0, ve[at[2]])
        ve[at[1]] = jnp.zeros((48, 128), F32)
    op.defect(re, ve, fe, 2, 5)
    k1 = [restrict(ke, 2 * q, 48, 0) * 0.125 for q in range(4)]
    s1 = [restrict(st, 2 * q, 48, 0) for q in (1, 2)]
    for ref, at in sides:
        put_near(ref, 1, re[at[2]])
        far = k1[2:] if at[0] == 0 else k1[:2]
        near, mid, last = (k1[1], s1[0], s1[1]) if at[0] == 0 else (k1[2], s1[1], s1[0])
        share = restrict_plane(re, at[3], 0)
        for n, v in enumerate((pack2(*far), pack2(near, mid), pack2(last, share))):
            ref[pl.ds(FINE_ROWS + 24 * n, 24), :] = v


def fine_kernel(
    k, f, s, above, below, xl, xr,
    slot, ve, re, tx, ty, tz, tzh, st, gain, t1x, t1y, t1z, t1h, s1, g1, f1,
    ke, fe, k1, v1, r1,
):
    zero = jnp.zeros((8, 128), F32)
    sub = rows(zero)
    for i, (target, ref) in enumerate(((ke, k), (fe, f), (st, s))):
        with_rows(target, ref, above, below, 8 * i, 8)
    sides = ((xl, (7, 6, 5)), (xr, (16, 17, 18)))

    def got(ref, n):
        return ref[pl.ds(48 * n, 48), :]

    def got_near(ref, n):
        at = 8 * 48 + 40 * n
        halo = ref[pl.ds(at + 32, 8), :]
        return jnp.concatenate([ref[pl.ds(at, 32), :], halo, halo], axis=0)

    for ref, at in sides:
        for n in range(3):
            ke[at[n]] = got(ref, n)
        for n in range(2):
            fe[at[n]] = got(ref, 3 + n)
            st[at[n]] = got(ref, 5 + n)
        ve[at[2]] = got(ref, 7)
    op = Level(0, tx, ty, tz, tzh, st, gain)
    op.build(ke, 6, 17)
    op.first_sweep(ve, fe, 6, 17)
    op.sweep(ve, fe, 6, 17)
    for ref, at in sides:
        ve[at[2]] = got_near(ref, 0)
    op.defect(re, ve, fe, 6, 17)
    re[5] = got_near(xl, 1) + tx[6] * ve[6]
    re[18] = got_near(xr, 1) + tx[18] * ve[17]
    for q in range(3, 9):
        k1[q] = restrict(ke, 2 * q, 48, 0) * 0.125
        s1[q] = restrict(st, 2 * q, 48, 0)
        f1[q] = restrict(re, 2 * q, 48, 0)
    for ref, lone, far, k2, s2 in ((xl, 5, (0, 1), 2, 1), (xr, 18, (10, 11), 9, 10)):
        a, b, c = (split(ref[pl.ds(FINE_ROWS + 24 * n, 24), :], 1) for n in range(3))
        k1[far[0]], k1[far[1]] = a
        k1[k2], s1[k2] = b
        s1[s2] = c[0]
        f1[k2] = c[1] + restrict_plane(re, lone, 0)
    op = Level(1, t1x, t1y, t1z, t1h, s1, g1)
    op.build(k1, 1, 10)
    op.first_sweep(v1, f1, 2, 9)
    op.sweep(v1, f1, 3, 8)
    op.defect(r1, v1, f1, 4, 7)
    source = [restrict(r1, 4 + 2 * p, 16, 1) for p in range(2)]
    perm = [restrict(k1, 4 + 2 * p, 16, 1) * 0.125 for p in range(2)]
    store = [restrict(s1, 4 + 2 * p, 16, 1) for p in range(2)]
    tiles = [pack4(*source, *perm), pack4(*store, *store), zero, zero, zero]
    for peer in range(16):
        for i, t in enumerate(tiles):
            slot[peer, i] = t
    j = lax.axis_index("gy")
    x = lax.axis_index("gx") % 4
    after, before = (j + 1) % 4, (j + 3) % 4
    first, last = pl.ds(0, 8), pl.ds(8, 8)
    for step, p, q in ((1, 5, 6), (3, 6, 4)):
        to = 4 * ((x + step) % 4)
        slot[to + j, 2] = pack2(r1[5, first, :], r1[6, first, :])
        slot[to + j, 3] = pack2(r1[5, last, :], r1[6, last, :])
        slot[to + j, 4] = pack2(f1[p, first, :], f1[p, last, :])
        slot[to + after, 2] = pack2(r1[q, last, :], r1[q + 1, last, :])
        slot[to + before, 2] = pack2(r1[q, first, :], r1[q + 1, first, :])
    for n in range(2):
        p = 4 + 2 * n
        r = pack2(r1[p, last, :], r1[p + 1, last, :])
        f = pack2(f1[p, last, :], f1[p + 1, last, :])
        slot[4 * x + after, 2 + n] = jnp.where(sub < 4, roll(f, -4, 0), r)
        r = pack2(r1[p, first, :], r1[p + 1, first, :])
        f = pack2(f1[p, first, :], f1[p + 1, first, :])
        slot[4 * x + before, 2 + n] = jnp.where(sub < 4, r, roll(f, 4, 0))


EDGE = 19
TO_NEXT = ((2, 6), (1, 7), (2, 6))
TO_PREV = ((0, 6), (0, 7), (0, 6))


def ring_kernel(g, own, to_next, to_prev):
    for x in range(4):
        t = [g[4 * x + j, 0] for j in range(4)]
        e0, o0 = exchange(t[0], t[1], 1)
        e1, o1 = exchange(t[2], t[3], 1)
        f0, k0 = exchange(e0, e1, 2)
        f1, k1 = exchange(o0, o1, 2)
        t = [g[4 * x + j, 1] for j in range(4)]
        e0, o0 = exchange(t[0], t[1], 1)
        e1, o1 = exchange(t[2], t[3], 1)
        s0 = jnp.where(bit(e0, 2), e0, e1)
        s1 = jnp.where(bit(o0, 2), o0, o1)
        for at, v in ((0, f0), (1, f1), (8, k0), (9, k1), (16, s0), (17, s1)):
            own[at + 2 * x] = v
    for out, parts in ((to_next, TO_NEXT), (to_prev, TO_PREV)):
        n = 0
        for i, (first, count) in enumerate(parts):
            for p in range(first, first + count):
                out[n] = own[8 * i + p]
                n += 1
    j = lax.axis_index("gy")
    x = lax.axis_index("gx") % 4
    for out, step in ((to_next, 3), (to_prev, 1)):
        at = 4 * ((x + step) % 4)
        for i in range(3):
            out[EDGE + i] = g[at + j, 2 + i]
        out[EDGE + 3] = g[at + (j + 1) % 4, 2]
        out[EDGE + 4] = g[at + (j + 3) % 4, 2]


def coarse_kernel(
    prev, own, nxt, msg, tx, ty, tyh, tz, tzh, st, gain, v2, r2, ke, fe
):
    whole = ((0, 8),) * 3
    for b, (ref, parts) in enumerate(((prev, TO_NEXT), (own, whole), (nxt, TO_PREV))):
        n = 0
        for target, (first, count) in zip((fe, ke, st), parts):
            for p in range(first, first + count):
                target[8 * b + p] = ref[n]
                n += 1
    op = Level(2, tx, ty, tz, tzh, st, gain, tyh)
    z = lax.axis_index("gx") // 4
    op.build(ke, 2, 21, 8 * z - 8, 2 * lax.axis_size("gx"))
    op.first_sweep(v2, fe, 2, 21)
    op.sweep(v2, fe, 3, 20)
    op.defect(r2, v2, fe, 4, 19)
    for i, (ref, scale) in enumerate(((r2, None), (ke, 0.125), (st, None))):
        cells = [restrict_packed(ref, 4 + 2 * c) for c in range(8)]
        if scale is not None:
            cells = [c * scale for c in cells]
        msg[2 * i] = pack_coarse(*cells[:4])
        msg[2 * i + 1] = pack_coarse(*cells[4:])


def halo_kernel(slots, prev, nxt, f1, tx, ty, tz, th, st, gain, v, q1, fe):
    zero = jnp.zeros((8, 128), F32)
    sub = rows(zero)
    j = lax.axis_index("gy")
    x = lax.axis_index("gx") % 4
    after, before = (j + 1) % 4, (j + 3) % 4
    first, last, halo = pl.ds(0, 8), pl.ds(8, 8), pl.ds(16, 8)

    def beside(step, outer):
        at = 4 * jnp.clip(x + step, 0, 3)
        inside = (x + step >= 0) & (x + step < 4)
        tiles = ((j, 2), (j, 3), (j, 4), (after, 2), (before, 2))
        return [
            split(jnp.where(inside, slots[at + y, t], outer[EDGE + n]), 1)
            for n, (y, t) in enumerate(tiles)
        ]

    left, right = beside(-1, prev), beside(1, nxt)
    ends = []
    for n in range(2):
        ends.append((split(slots[4 * x + after, 2 + n], 1), split(slots[4 * x + before, 2 + n], 1)))
    for q in range(2, 10):
        fe[q] = f1[q]
    for q in range(4, 8):
        a, b = (e[q % 2] for e in ends[(q - 4) // 2])
        fe[q, halo, :] = jnp.where(
            sub == 2, roll(a, -4, 0), jnp.where(sub == 5, roll(b, 4, 0), f1[q, halo, :])
        )
    for q, side in ((1, left), (10, right)):
        fe[q, first, :], fe[q, last, :] = side[2]
        fe[q, halo, :] = zero
    op = Level(1, tx, ty, tz, th, st, gain)
    op.first_sweep(v, fe, 1, 10)
    op.sweep(v, fe, 2, 9)
    op.defect(q1, v, fe, 3, 8)
    for q in range(4, 8):
        a, b = (e[q % 2] for e in ends[(q - 4) // 2])
        near = (sub == 1) | (sub == 2)
        q1[q, halo, :] = jnp.where(
            near, a, jnp.where((sub == 5) | (sub == 6), b, q1[q, halo, :])
        )
    for side, q, edge, corner in ((left, 1, 1, 2), (right, 9, 10, 8)):
        for n in range(2):
            q1[q + n, first, :] = side[0][n]
            q1[q + n, last, :] = side[1][n]
        for n in range(2):
            q1[corner + n, halo, :] = jnp.where(sub < 4, side[3][n], side[4][n])
        q1[edge, halo, :] = zero


def up_kernel(
    own3, left3, right3,
    t2x, t2y, t2yh, t2z, t2h, s2, g2, v2, r2,
    t1x, t1y, t1z, t1h, s1, g1,
    t0x, t0y, t0z, t0h, s0, g0, v0, r0,
    w1, q1,
    pressure, residual,
    k3, f3, s3, t3x, t3y, t3yh, t3z, t3h, g3, v3, c2, e2, c1, dup, c0, pv, rv, sems,
):
    n = 0
    for ref in (left3, own3, right3):
        for half in range(2):
            for i, target in enumerate((f3, k3, s3)):
                for c, v in enumerate(unpack_coarse(ref[2 * i + half])):
                    target[n + c] = v
            n += 4
    i = lax.axis_index("gx")
    j = lax.axis_index("gy")
    z, x = i // 4, i % 4
    op = Level(3, t3x, t3y, t3z, t3h, s3, g3, t3yh)
    op.build(k3, 1, 22, 4 * z - 10, lax.axis_size("gx"))
    op.first_sweep(v3, f3, 1, 22)
    for m in range(1, COARSE):
        op.sweep(v3, f3, 1 + m, 22 - m)
    for n in range(8, 16):
        e = v3[n]
        c2[2 * n - 12] = e
        c2[2 * n - 11] = e
    op = Level(2, t2x, t2y, t2z, t2h, s2, g2, t2yh)
    op.sweep(c2, r2, 5, 18)
    op.sweep(c2, r2, 6, 17)
    for p in range(6, 18):
        e2[p] = v2[p] + c2[p]
    sub = rows(jnp.zeros((8, 128), F32))
    for p in range(6):
        e = e2[6 + 2 * x + p]
        part = []
        for step in (0, 1, -1):
            t = jnp.where((lanes(e) & 3) == j + step, e, 0.0)
            t = t + swap(t, 1)
            part.append(t + swap(t, 2))
        for n, t in enumerate(part):
            doubled(dup, n, t)
        halo = jnp.where(sub < 4, dup[1, pl.ds(0, 8), :], dup[2, pl.ds(8, 8), :])
        for q in (2 * p, 2 * p + 1):
            c1[q, pl.ds(0, 16), :] = dup[0]
            c1[q, pl.ds(16, 8), :] = halo

    op = Level(1, t1x, t1y, t1z, t1h, s1, g1)
    op.sweep(c1, q1, 1, 10)
    op.sweep(c1, q1, 2, 9)
    for q in range(2, 10):
        e = w1[q] + c1[q]
        doubled(c0, 2 * q, e)
        doubled(c0, 2 * q + 1, e)
    op = Level(0, t0x, t0y, t0z, t0h, s0, g0)
    op.sweep(c0, r0, 6, 17)
    op.sweep(c0, r0, 7, 16)

    copies = []

    def use(p, here, out):
        n = p - 8
        pv[n] = v0[p, pl.ds(0, 32), :] + here[:32]
        rv[n] = r0[p, pl.ds(0, 32), :] - out[:32]
        if n % 2 == 1:
            two = pl.ds(n - 1, 2)
            for m, (src, dst) in enumerate(((pv, pressure), (rv, residual))):
                c = pltpu.make_async_copy(src.at[two], dst.at[two], sems.at[n - m])
                c.start()
                copies.append(c)

    op.apply(c0, 8, 15, use)
    for c in copies:
        c.wait()


def call(kernel, outs, scratch, args):
    return pl.pallas_call(
        kernel,
        out_shape=[jax.ShapeDtypeStruct(s, F32) for s in outs],
        scratch_shapes=[pltpu.VMEM(s, F32) for s in scratch],
        compiler_params=PARAMS,
    )(*args)


def shifted(x, axis, k):
    n = lax.axis_size(axis)
    return lax.ppermute(x, axis, [(i, i + k) for i in range(n) if 0 <= i + k < n])


def turned(x, axis, k):
    n = lax.axis_size(axis)
    return lax.ppermute(x, axis, [(i, (i + k) % n) for i in range(n)])


def body(permeability, storage, source_term):
    k, s, f = permeability, storage, source_term
    parts = (f[:, :8], s[:, :8], f[:, 24:], s[:, 24:])
    (fa, sa, fb, sb), kk = lax.optimization_barrier((parts, k))
    above = shifted(jnp.concatenate([kk[:, :8], fa, sa]), "gy", -1)
    below = shifted(jnp.concatenate([kk[:, 24:], fb, sb]), "gy", 1)
    own = (kk, f, s, above, below)
    to_left, to_right = call(
        own_kernel, [(MESSAGE_ROWS, 128)] * 2, [(8, 48, 128)] * 10, own
    )
    xl, xr = shifted(to_right, "gx", 1), shifted(to_left, "gx", -1)
    fine, mid = (24, 48, 128), (12, 24, 128)
    slot, v0, r0, t0x, t0y, t0z, t0h, s0, g0, t1x, t1y, t1z, t1h, s1, g1, f1 = call(
        fine_kernel,
        [(16, 5, 8, 128)] + [fine] * 8 + [mid] * 7,
        [fine] * 2 + [mid] * 3,
        own + (xl, xr),
    )
    n = lax.axis_size("gx") * lax.axis_size("gy")
    groups = [[16 * a + b for b in range(16)] for a in range(n // 16)]
    slots = lax.all_to_all(slot, ("gx", "gy"), 0, 0, axis_index_groups=groups)
    ring, to_next, to_prev = call(ring_kernel, [(24, 8, 128)] * 3, [], (slots,))
    prev, nxt = turned(to_next, "gx", 4), turned(to_prev, "gx", -4)
    low = (24, 8, 128)
    msg3, t2x, t2y, t2yh, t2z, t2h, s2, g2, v2, r2 = call(
        coarse_kernel, [(6, 8, 128)] + [low] * 9, [low] * 2, (prev, ring, nxt)
    )
    w1, q1 = call(
        halo_kernel, [mid] * 2, [mid], (slots, prev, nxt, f1, t1x, t1y, t1z, t1h, s1, g1)
    )
    left3, right3 = turned(msg3, "gx", 8), turned(msg3, "gx", -8)
    own = (8, 32, 128)
    scratch = [low] * 12 + [mid, (3, 16, 128), fine, own, own]
    args = (
        msg3, left3, right3,
        t2x, t2y, t2yh, t2z, t2h, s2, g2, v2, r2,
        t1x, t1y, t1z, t1h, s1, g1,
        t0x, t0y, t0z, t0h, s0, g0, v0, r0,
        w1, q1,
    )
    return tuple(pl.pallas_call(
        up_kernel,
        out_shape=[jax.ShapeDtypeStruct(own, F32)] * 2,
        out_specs=[pl.BlockSpec(memory_space=pl.ANY)] * 2,
        scratch_shapes=[pltpu.VMEM(n, F32) for n in scratch] + [pltpu.SemaphoreType.DMA((8,))],
        compiler_params=PARAMS,
    )(*args))


def solution(mesh):
    spec = P(("ma", "gx"), "gy", None)
    return jax.shard_map(
        body, mesh=mesh, in_specs=(spec,) * 3, out_specs=(spec,) * 2, check_vma=False
    )
```
